256 devices in a mesh: slab: 64 (over z, x, core), coil: 4 (over y).
Axes of the slice: x: 4, y: 4, z: 8, core: 2. Of those that a mesh axis runs over, the one named last changes fastest.
Arguments:
- raw_data: bfloat16 [2, 64, 64, 512, 256], P(None, None, 'slab', 'coil'), may hold values from -6 to 6
- gcc_matrix: bfloat16 [2, 64, 16, 64], P(None, 'slab'), may hold values from -0.5 to 0.5
- sens_maps: bfloat16 [2, 16, 64, 512, 256], P(None, 'coil', None, 'slab'), may hold values from -24 to 24
- line_mask: int32 [512, 256], replicated, may hold values 0 or 1
Outputs:
- solution: float32 [2, 64, 512, 256], P(None, None, 'slab')
- residual: float32 [2, 64, 512, 256], P(None, None, 'slab')
The draws below stay inside these ranges and needn't reach their ends.
All inputs are finite; a program needn't handle non-finite values.
Results may differ from the reference program's by a relative error of at most 0.034.
Values may be sent and summed in bfloat16 or wider, within the bound.
A program may use at most 128 MiB of HBM per device.

```python
import math
import jax
import jax.numpy as jnp
from jax import lax

NRAW = 64
NV = 16
NY = 512
NZ = 256
ITERS = 2
X = 64


def draw_sens_maps(key, part):
    key = jax.random.fold_in(key, 7)
    base_key, row_key, column_key = jax.random.split(key, 3)
    shape = (2, NV, X, NY, NZ)
    row_scale = jnp.exp(jax.random.uniform(row_key, (1, 1, 1, NY, 1), jnp.float32, math.log(0.25), math.log(2.5)))
    column_scale = jnp.exp(jax.random.uniform(column_key, (1, 1, X, 1, 1), jnp.float32, math.log(0.5), math.log(1.5)))
    placing = jnp.arange(NY, dtype=jnp.float32).reshape(1, 1, 1, NY, 1) / float(max(NY - 1, 1))
    base = jnp.clip(jax.random.normal(base_key, shape, jnp.float32), -4.0, 4.0)
    rising = 1.0 + 2.0 * placing
    return (0.35 * base * row_scale * column_scale * rising).astype(jnp.bfloat16)


def plant(array, stream_key, smallest, top_value):
    place = [jax.random.randint(jax.random.fold_in(stream_key, axis), (), 0, length) for axis, length in enumerate(array.shape)]
    longest = array.shape.index(max(array.shape))
    neighbour = place[:longest] + [(place[longest] + 1) % array.shape[longest]] + place[longest + 1:]
    return array.at[tuple(place)].set(smallest).at[tuple(neighbour)].set(top_value)


def block_scale(stream_key, dims, pieces, smallest, top_value):
    loudness, own = 1.0, jax.random.fold_in(stream_key, 6)
    for axis_at, blocks in pieces:
        heights = jnp.exp(jax.random.uniform(jax.random.fold_in(own, axis_at), (blocks,), jnp.float32, smallest / len(pieces), top_value / len(pieces)))
        loudness = loudness * jnp.repeat(heights, dims[axis_at] // blocks).reshape([-1 if axis == axis_at else 1 for axis in range(len(dims))])
    return loudness


def centred(stream_key, dims, width, reach, cuts=(), kind=jnp.bfloat16):
    entries = width * jax.random.normal(stream_key, dims, jnp.float32)
    if cuts:
        entries = entries * block_scale(stream_key, dims, cuts, -0.22, 0.18)
    return jnp.clip(entries, -reach, reach).astype(kind)


def setup_inputs(seed: int = 0) -> dict:
    seeds = jax.random.split(jax.random.key(seed), 5)
    return {
        "raw_data": centred(seeds[0], (2, NRAW, X, NY, NZ), 1.0, 6.0, ((2, 64), (3, 4))),
        "gcc_matrix": centred(seeds[1], (2, X, NV, NRAW), (2 * NRAW) ** -0.5, 0.5, ((1, 64),)),
        "sens_maps": draw_sens_maps(jax.random.fold_in(seeds[4], 71), 0),
        "line_mask": plant((jax.random.randint(seeds[3], (NY, NZ), 0, 3) < 1).astype(jnp.int32), jax.random.fold_in(seeds[3], 1), 0, 1),
    }


ridge = 0.5

def dft_tables(length, direction_sign):
    positions = jnp.arange(length, dtype=jnp.int32)
    phase_int = positions[:, None] * positions[None, :] % length
    angles = phase_int.astype(jnp.float32) * (2.0 * math.pi / length)
    scale_norm = 1.0 / math.sqrt(length)
    cosine = jnp.cos(angles) * scale_norm
    sine = jnp.sin(angles) * (direction_sign * scale_norm)
    return (cosine.astype(jnp.bfloat16), (sine - cosine).astype(jnp.bfloat16), (cosine + sine).astype(jnp.bfloat16))

def along_last(source, matrix):
    return jnp.einsum('...j,jk->...k', source.astype(jnp.float32), matrix.astype(jnp.float32))

def along_rows(source, matrix):
    return jnp.einsum('...jz,jk->...kz', source.astype(jnp.float32), matrix.astype(jnp.float32))

def transform(real_part, imag_part, table_set, applier):
    cosine, minus_cos, plus_cos = table_set
    merged = (real_part.astype(jnp.float32) + imag_part.astype(jnp.float32)).astype(jnp.bfloat16)
    common = applier(merged, cosine)
    return (common - applier(imag_part, plus_cos), common + applier(real_part, minus_cos))

def rounded(parts):
    return jnp.stack([parts[0], parts[1]]).astype(jnp.bfloat16)

def coil_images(volume, coil_maps):
    real_part = coil_maps[0] * volume[0][None] - coil_maps[1] * volume[1][None]
    imag_part = coil_maps[0] * volume[1][None] + coil_maps[1] * volume[0][None]
    return rounded((real_part, imag_part))

def kspace_round(source, mask_values, forward_rows, inverse_rows, applier):
    spectral = transform(source[0], source[1], forward_rows, applier)
    masked = rounded((spectral[0] * mask_values, spectral[1] * mask_values))
    return rounded(transform(masked[0], masked[1], inverse_rows, applier))

def combine(source, coil_maps, inverse_depth, applier):
    real_part, imag_part = transform(source[0], source[1], inverse_depth, applier)
    summed_real = lax.optimization_barrier(jnp.sum(coil_maps[0] * real_part + coil_maps[1] * imag_part, axis=0))
    summed_imag = lax.optimization_barrier(jnp.sum(coil_maps[0] * imag_part - coil_maps[1] * real_part, axis=0))
    return jnp.stack([summed_real, summed_imag])

def mix_coils(left_side, right_hand):
    return jnp.einsum('vr,ryz->vyz', left_side.astype(jnp.float32), right_hand.astype(jnp.float32))

def reference(raw_data, gcc_matrix, sens_maps, line_mask):
    rows_total, depth_len = line_mask.shape
    forward_depth = dft_tables(depth_len, -1.0)
    inverse_depth = dft_tables(depth_len, 1.0)
    forward_rows = dft_tables(rows_total, -1.0)
    inverse_rows = dft_tables(rows_total, 1.0)
    mask_values = line_mask.astype(jnp.float32)
    positions = jnp.arange(raw_data.shape[2], dtype=jnp.int32)

    def slice_maps(position):
        return lax.dynamic_index_in_dim(sens_maps, position, 2, keepdims=False)

    def right_slice(position):
        raw_slice = lax.dynamic_index_in_dim(raw_data, position, 2, keepdims=False)
        gcc_slice = lax.dynamic_index_in_dim(gcc_matrix, position, 1, keepdims=False)
        compressed = rounded((mix_coils(gcc_slice[0], raw_slice[0]) - mix_coils(gcc_slice[1], raw_slice[1]), mix_coils(gcc_slice[0], raw_slice[1]) + mix_coils(gcc_slice[1], raw_slice[0])))
        masked_data = rounded((compressed[0] * mask_values, compressed[1] * mask_values))
        data_rows = rounded(transform(masked_data[0], masked_data[1], inverse_rows, along_rows))
        return combine(data_rows, slice_maps(position), inverse_depth, along_last)

    def normal_slice(inputs):
        position, direction_slice = inputs
        coil_maps = slice_maps(position)
        images = coil_images(direction_slice, coil_maps)
        spectra = rounded(transform(images[0], images[1], forward_depth, along_last))
        returned = kspace_round(spectra, mask_values, forward_rows, inverse_rows, along_rows)
        return combine(returned, coil_maps, inverse_depth, along_last)

    def normal(direction):
        mapped = lax.map(normal_slice, (positions, jnp.moveaxis(direction, 1, 0)))
        return jnp.moveaxis(mapped, 0, 1) + ridge * direction
    right_side = jnp.moveaxis(lax.map(right_slice, positions), 0, 1)
    solution = jnp.zeros_like(right_side)
    residual = right_side
    direction = right_side
    norm_now = jnp.sum(residual * residual)
    for iteration in range(ITERS):
        applied = normal(direction)
        step_size = norm_now / jnp.sum(direction * applied)
        solution = solution + step_size * direction
        residual = residual - step_size * applied
        norm_next = jnp.sum(residual * residual)
        direction = residual + norm_next / norm_now * direction
        norm_now = norm_next
    return (solution, residual)
```

```python
import math

import jax
import jax.numpy as jnp
import ml_dtypes
import numpy as np
from jax import lax
from jax.experimental import pallas as pl
from jax.experimental.pallas import tpu as pltpu
from jax.sharding import PartitionSpec as P

MESH = pl.DeviceIdType.MESH
BF16 = jnp.bfloat16
F32 = jnp.float32

RIDGE = 0.5
SLABS = 64
GROUPS = 4
COILS = 4
ROWS = 512
DEPTH = 256
CHUNKS = 4
CHUNK = ROWS // CHUNKS
BLOCKS = SLABS // CHUNKS


def place(slab):
    return lax.rem(lax.div(slab, 2), 4) * 16 + lax.div(slab, 8) * 2 + lax.rem(slab, 2)


def tables():
    def cos_sin(length):
        index = np.arange(length, dtype=np.int64)
        angle = (index[:, None] * index[None, :] % length) * (2.0 * math.pi / length)
        return np.cos(angle) / math.sqrt(length), np.sin(angle) / math.sqrt(length)

    slab = np.arange(SLABS)
    position = ((slab // 2) % 4) * 16 + (slab // 8) * 2 + slab % 2
    order = np.zeros(SLABS, np.int64)
    order[position] = slab
    rows = (order[:, None] * 8 + np.arange(8)[None, :]).reshape(-1)
    cosine, sine = cos_sin(ROWS)
    cosine, sine = cosine[:, rows], sine[:, rows]
    rows_forward = np.block([[cosine, sine], [-sine, cosine]])
    rows_inverse = np.block([[cosine.T, -sine.T], [sine.T, cosine.T]])
    cosine, sine = cos_sin(DEPTH)
    depth_forward = np.block([[cosine, -sine], [sine, cosine]])
    depth_inverse = np.block([[cosine, sine], [-sine, cosine]])
    return [
        jnp.asarray(table.astype(ml_dtypes.bfloat16))
        for table in (rows_forward, rows_inverse, depth_forward, depth_inverse)
    ]


def dot(left, right):
    return jnp.dot(left, right, preferred_element_type=F32)


def kernel(
    comp_hbm, sens_hbm, mask_hbm, rf_hbm, ri_hbm, df_hbm, di_hbm,
    sol_ref, res_ref,
    kd, sb, mask, rf, ri, df, di,
    zbuf, mbuf, fold, lhs,
    part, got1, sum1, got2, cs, rowbuf,
    ysc, zsc, tile,
    load_sem, kd_send, kd_recv, sb_send, sb_recv,
    p1_send, p1_recv, p2_send, p2_recv, p3_send, p3_recv,
    rb_send, rb_recv, ys_send, ys_recv, zs_send, zs_recv,
):
    me = lax.axis_index("slab")
    group = lax.axis_index("coil")
    my_place = place(me)
    side_a = group + 1 - 2 * lax.rem(group, 2)
    side_b = 3 - group
    half_a = lax.rem(lax.div(group + 1, 2), 2)
    half_b = lax.div(group, 2)

    barrier = pltpu.get_barrier_semaphore()

    def greet(step, carry):
        peer = lax.rem(me + step, SLABS)
        pl.semaphore_signal(barrier, inc=1, device_id=(peer, group), device_id_type=MESH)
        return carry

    lax.fori_loop(1, SLABS, greet, 0)
    for step in range(1, GROUPS):
        pl.semaphore_signal(
            barrier, inc=1, device_id=(me, lax.rem(group + step, GROUPS)), device_id_type=MESH
        )

    own_loads = [
        pltpu.make_async_copy(comp_hbm.at[:, pl.ds(COILS * group, COILS)],
                              kd.at[:, :, pl.ds(CHUNK * group, CHUNK), :], load_sem.at[0]),
        pltpu.make_async_copy(ri_hbm, ri, load_sem.at[1]),
        pltpu.make_async_copy(mask_hbm, mask, load_sem.at[2]),
        pltpu.make_async_copy(sens_hbm.at[:, me], sb.at[:, my_place], load_sem.at[3]),
        pltpu.make_async_copy(di_hbm, di, load_sem.at[4]),
        pltpu.make_async_copy(df_hbm, df, load_sem.at[5]),
        pltpu.make_async_copy(rf_hbm, rf, load_sem.at[6]),
    ]
    for load in own_loads:
        load.start()

    pl.semaphore_wait(barrier, SLABS - 1 + GROUPS - 1)

    for step in range(1, GROUPS):
        peer = lax.rem(group + step, GROUPS)
        pltpu.make_async_remote_copy(
            src_ref=comp_hbm.at[:, pl.ds(COILS * peer, COILS)],
            dst_ref=kd.at[:, :, pl.ds(CHUNK * group, CHUNK), :],
            send_sem=kd_send, recv_sem=kd_recv,
            device_id=(me, peer), device_id_type=MESH,
        ).start()

    def send_maps(step, carry):
        peer = lax.rem(me + step, SLABS)
        pltpu.make_async_remote_copy(
            src_ref=sens_hbm.at[:, peer], dst_ref=sb.at[:, my_place],
            send_sem=sb_send, recv_sem=sb_recv,
            device_id=(peer, group), device_id_type=MESH,
        ).start()
        return carry

    lax.fori_loop(1, SLABS, send_maps, 0)

    def settle(ref, sem):
        pltpu.make_async_copy(ref, ref, sem).wait()

    for load in own_loads[:3]:
        load.wait()
    settle(kd.at[:, :, pl.ds(0, CHUNK * 3), :], kd_recv)

    def inverse_rows(coil):
        for half in range(2):
            out = dot(ri[half * ROWS:(half + 1) * ROWS, :], mbuf[...])
            fold[coil, :, half * DEPTH:(half + 1) * DEPTH] = out.astype(BF16)

    def data_coil(coil, carry):
        for half in range(2):
            mbuf[half * ROWS:(half + 1) * ROWS, :] = kd[half, coil] * mask[...]
        inverse_rows(coil)
        return carry

    lax.fori_loop(0, COILS, data_coil, 0)
    for load in own_loads[3:]:
        load.wait()
    settle(sb.at[:, pl.ds(0, SLABS - 1)], sb_recv)

    def maps_of(coil, chunk):
        both = sb[coil, pl.ds(chunk * BLOCKS, BLOCKS)].astype(F32)
        return both[:, :8].reshape(CHUNK, DEPTH), both[:, 8:].reshape(CHUNK, DEPTH)

    def piece(chunk, way, half):
        return pl.ds(chunk * BLOCKS + way * 8 + half * 4, 4)

    def coil_sum(turn, between=None):
        ways = ((0, half_a, side_a, side_b), (1, half_b, side_b, side_a))

        def combine(chunk, carry):
            source = fold[:, pl.ds(chunk * CHUNK, CHUNK), :].reshape(COILS * CHUNK, 2 * DEPTH)
            out = dot(source, di[...])
            real = imag = None
            for coil in range(COILS):
                a = out[coil * CHUNK:(coil + 1) * CHUNK, :DEPTH]
                b = out[coil * CHUNK:(coil + 1) * CHUNK, DEPTH:]
                sr, si = maps_of(coil, chunk)
                re, im = sr * a + si * b, sr * b - si * a
                real = re if real is None else real + re
                imag = im if imag is None else imag + im
            packed = jnp.concatenate(
                [real.reshape(BLOCKS, 8, DEPTH), imag.reshape(BLOCKS, 8, DEPTH)], axis=1
            )
            part[turn, pl.ds(chunk * BLOCKS, BLOCKS)] = packed.astype(BF16)
            for way, half, first, second in ways:
                pltpu.make_async_remote_copy(
                    src_ref=part.at[turn, piece(chunk, way, 1 - half)],
                    dst_ref=got1.at[turn, chunk, way],
                    send_sem=p1_send.at[turn], recv_sem=p1_recv.at[turn, chunk, way],
                    device_id=(me, first), device_id_type=MESH,
                ).start()
            return carry

        lax.fori_loop(0, CHUNKS, combine, 0)
        if between is not None:
            between()

        def second_step(chunk, carry):
            for way, half, first, second in ways:
                settle(got1.at[turn, chunk, way], p1_recv.at[turn, chunk, way])
                mine = part[turn, piece(chunk, way, half)].astype(F32)
                sum1[turn, chunk, way] = (mine + got1[turn, chunk, way].astype(F32)).astype(BF16)
                pltpu.make_async_remote_copy(
                    src_ref=sum1.at[turn, chunk, way], dst_ref=got2.at[turn, chunk, way],
                    send_sem=p2_send.at[turn], recv_sem=p2_recv.at[turn, chunk, way],
                    device_id=(me, second), device_id_type=MESH,
                ).start()
            return carry

        lax.fori_loop(0, CHUNKS, second_step, 0)

        def third_step(chunk, carry):
            for way, half, first, second in ways:
                settle(got2.at[turn, chunk, way], p2_recv.at[turn, chunk, way])
                whole = sum1[turn, chunk, way].astype(F32) + got2[turn, chunk, way].astype(F32)
                cs[turn, piece(chunk, way, half)] = whole.astype(BF16)
                pltpu.make_async_remote_copy(
                    src_ref=cs.at[turn, piece(chunk, way, half)],
                    dst_ref=cs.at[turn, piece(chunk, way, half)],
                    send_sem=p3_send.at[turn], recv_sem=p3_recv.at[turn, chunk, way],
                    device_id=(me, first), device_id_type=MESH,
                ).start()
            return carry

        lax.fori_loop(0, CHUNKS, third_step, 0)

    def receive_chunk(turn, chunk):
        for way, half in ((0, half_a), (1, half_b)):
            settle(cs.at[turn, piece(chunk, way, 1 - half)], p3_recv.at[turn, chunk, way])

    def send_rows(turn, chunk):
        def send(step, carry):
            to = lax.rem(my_place + step, BLOCKS)
            peer = lax.div(to, 2) * 8 + chunk * 2 + lax.rem(to, 2)

            @pl.when(peer != me)
            def _():
                pltpu.make_async_remote_copy(
                    src_ref=cs.at[turn, chunk * BLOCKS + to], dst_ref=rowbuf.at[turn, me],
                    send_sem=rb_send.at[turn], recv_sem=rb_recv.at[turn],
                    device_id=(peer, group), device_id_type=MESH,
                ).start()

            return carry

        lax.fori_loop(0, BLOCKS, send, 0)

    def image(turn, chunk):
        both = cs[turn, pl.ds(chunk * BLOCKS, BLOCKS)].astype(F32)
        return both[:, :8].reshape(CHUNK, DEPTH), both[:, 8:].reshape(CHUNK, DEPTH)

    def fold_rows(values):
        return jnp.sum(values.reshape(-1, 8, DEPTH), axis=0)

    def total(values):
        return jnp.sum(values, keepdims=True)

    def spread_groups(turn, value):
        ysc[turn, group] = jnp.broadcast_to(value, (8, 128))
        for step in range(1, GROUPS):
            peer = lax.rem(group + step, GROUPS)
            pltpu.make_async_remote_copy(
                src_ref=ysc.at[turn, group], dst_ref=ysc.at[turn, group],
                send_sem=ys_send.at[turn], recv_sem=ys_recv.at[turn],
                device_id=(me, peer), device_id_type=MESH,
            ).start()

    def spread_slabs(turn, values):
        settle(ysc.at[turn, pl.ds(0, GROUPS - 1)], ys_recv.at[turn])
        spectral = jnp.sum(ysc[turn], axis=0)
        row = lax.broadcasted_iota(jnp.int32, (8, 128), 0)
        for index, value in enumerate(values):
            spectral = jnp.where(row == index + 1, jnp.broadcast_to(value, (8, 128)), spectral)
        tile[turn] = spectral
        zsc[turn, me] = spectral

        def send(step, carry):
            peer = lax.rem(me + step, SLABS)
            pltpu.make_async_remote_copy(
                src_ref=tile.at[turn], dst_ref=zsc.at[turn, me],
                send_sem=zs_send.at[turn], recv_sem=zs_recv.at[turn],
                device_id=(peer, group), device_id_type=MESH,
            ).start()
            return carry

        lax.fori_loop(1, SLABS, send, 0)

    def collect(turn):
        settle(zsc.at[turn, pl.ds(0, SLABS - 1)], zs_recv.at[turn])
        summed = jnp.sum(zsc[turn], axis=0)
        return [summed[index:index + 1, 0:1] for index in range(3)]

    zero = jnp.zeros((8, DEPTH), F32)
    coil_sum(0)
    alpha = None
    for turn in range(2):

        def front(chunk, carry):
            receive_chunk(turn, chunk)
            send_rows(turn, chunk)
            pr, pi = image(0, chunk)
            if turn == 1:
                ar, ai = image(1, chunk)
                ar, ai = ar + RIDGE * pr, ai + RIDGE * pi
                pr, pi = pr - alpha * ar, pi - alpha * ai
                carry = (carry[0], carry[1] + fold_rows(pr * ar + pi * ai))
            carry = (carry[0] + fold_rows(pr * pr + pi * pi), carry[1])
            for coil in range(COILS):
                sr, si = maps_of(coil, chunk)
                rows = pl.ds(coil * CHUNK, CHUNK)
                lhs[rows, :DEPTH] = (sr * pr - si * pi).astype(BF16)
                lhs[rows, DEPTH:] = (sr * pi + si * pr).astype(BF16)
            out = dot(lhs[...], df[...])
            for coil in range(COILS):
                rows = slice(coil * CHUNK, (coil + 1) * CHUNK)
                zbuf[coil, pl.ds(chunk * CHUNK, CHUNK), :] = out[rows, :DEPTH].astype(BF16)
                zbuf[coil, pl.ds(ROWS + chunk * CHUNK, CHUNK), :] = out[rows, DEPTH:].astype(BF16)
            return carry

        norm, cross = lax.fori_loop(0, CHUNKS, front, (zero, zero))

        def rows_coil(coil, energy):
            for half in range(2):
                out = dot(rf[half * ROWS:(half + 1) * ROWS, :], zbuf[coil])
                weighted = out.astype(BF16) * mask[...]
                mbuf[half * ROWS:(half + 1) * ROWS, :] = weighted
                wide = weighted.astype(F32)
                energy = energy + fold_rows(wide * wide)
            inverse_rows(coil)
            return energy

        energy = lax.fori_loop(0, COILS, rows_coil, zero)
        spread_groups(turn, total(energy))
        coil_sum(turn + 1, lambda: spread_slabs(turn, (total(norm), total(cross))))
        if turn == 0:
            spectral, norm0, _ = collect(0)
            energy0 = spectral + RIDGE * norm0
            alpha = norm0 / energy0

    def last(chunk, carry):
        receive_chunk(2, chunk)
        send_rows(2, chunk)
        return carry

    lax.fori_loop(0, CHUNKS, last, 0)
    for turn in range(3):
        rowbuf[turn, me] = cs[turn, my_place]
    spectral, norm1, cross1 = collect(1)
    beta = norm1 / norm0
    energy1 = spectral + RIDGE * norm1 + 2.0 * beta * cross1 + beta * beta * energy0
    alpha1 = norm1 / energy1
    for turn in range(3):
        settle(rowbuf.at[turn, pl.ds(0, SLABS - 1)], rb_recv.at[turn])

    def finish(step, carry):
        some = pl.ds(step * 16, 16)
        first = rowbuf[0, some].astype(F32)
        applied = rowbuf[1, some].astype(F32) + RIDGE * first
        residual = first - alpha * applied
        again = rowbuf[2, some].astype(F32) + RIDGE * residual
        direction = residual + beta * first
        answer = alpha * first + alpha1 * direction
        left = residual - alpha1 * (again + beta * applied)
        for index in range(2):
            sol_ref[index, some] = answer[:, index * 8:index * 8 + 8]
            res_ref[index, some] = left[:, index * 8:index * 8 + 8]
        return carry

    lax.fori_loop(0, SLABS // 16, finish, 0)

    settle(kd.at[:, :, pl.ds(0, CHUNK * 3), :], kd_send)
    settle(sb.at[:, pl.ds(0, SLABS - 1)], sb_send)
    for turn in range(3):
        settle(cs.at[turn, pl.ds(0, SLABS // 2)], p1_send.at[turn])
        settle(cs.at[turn, pl.ds(0, SLABS // 2)], p2_send.at[turn])
        settle(cs.at[turn, pl.ds(0, SLABS // 2)], p3_send.at[turn])
        settle(rowbuf.at[turn, pl.ds(0, SLABS - 1)], rb_send.at[turn])
    for turn in range(2):
        settle(ysc.at[turn, pl.ds(0, GROUPS - 1)], ys_send.at[turn])
        settle(zsc.at[turn, pl.ds(0, SLABS - 1)], zs_send.at[turn])


def shards(raw_data, gcc_matrix, sens_maps, line_mask):
    real, imag = gcc_matrix[0, 0], gcc_matrix[1, 0]
    mixing = jnp.concatenate(
        [jnp.concatenate([real, -imag], axis=1), jnp.concatenate([imag, real], axis=1)]
    )
    raw = raw_data.reshape(2 * 64, ROWS // GROUPS, DEPTH)
    compressed = jnp.einsum("mr,ryz->myz", mixing, raw, preferred_element_type=F32).astype(BF16)
    compressed = compressed.reshape(2, 16, ROWS // GROUPS, DEPTH)
    maps = jnp.transpose(sens_maps, (1, 2, 0, 3, 4)).reshape(COILS, SLABS, 16, DEPTH)
    mask = line_mask.astype(BF16)

    dma = pltpu.SemaphoreType.DMA
    out = jax.ShapeDtypeStruct((2, SLABS, 8, DEPTH), F32)
    return pl.pallas_call(
        kernel,
        out_shape=(out, out),
        in_specs=[pl.BlockSpec(memory_space=pl.ANY)] * 7,
        out_specs=(pl.BlockSpec(memory_space=pltpu.VMEM),) * 2,
        scratch_shapes=[
            pltpu.VMEM((2, COILS, ROWS, DEPTH), BF16),
            pltpu.VMEM((COILS, SLABS, 16, DEPTH), BF16),
            pltpu.VMEM((ROWS, DEPTH), BF16),
            pltpu.VMEM((2 * ROWS, 2 * ROWS), BF16),
            pltpu.VMEM((2 * ROWS, 2 * ROWS), BF16),
            pltpu.VMEM((2 * DEPTH, 2 * DEPTH), BF16),
            pltpu.VMEM((2 * DEPTH, 2 * DEPTH), BF16),
            pltpu.VMEM((COILS, 2 * ROWS, DEPTH), BF16),
            pltpu.VMEM((2 * ROWS, DEPTH), BF16),
            pltpu.VMEM((COILS, ROWS, 2 * DEPTH), BF16),
            pltpu.VMEM((COILS * CHUNK, 2 * DEPTH), BF16),
            pltpu.VMEM((3, SLABS, 16, DEPTH), BF16),
            pltpu.VMEM((3, CHUNKS, 2, 4, 16, DEPTH), BF16),
            pltpu.VMEM((3, CHUNKS, 2, 4, 16, DEPTH), BF16),
            pltpu.VMEM((3, CHUNKS, 2, 4, 16, DEPTH), BF16),
            pltpu.VMEM((3, SLABS, 16, DEPTH), BF16),
            pltpu.VMEM((3, SLABS, 16, DEPTH), BF16),
            pltpu.VMEM((2, GROUPS, 8, 128), F32),
            pltpu.VMEM((2, SLABS, 8, 128), F32),
            pltpu.VMEM((2, 8, 128), F32),
            dma((7,)), dma, dma, dma, dma,
            dma((3,)), dma((3, CHUNKS, 2)),
            dma((3,)), dma((3, CHUNKS, 2)),
            dma((3,)), dma((3, CHUNKS, 2)),
            dma((3,)), dma((3,)), dma((2,)), dma((2,)), dma((2,)), dma((2,)),
        ],
        compiler_params=pltpu.CompilerParams(
            collective_id=0, has_side_effects=True, vmem_limit_bytes=48 * 1024 * 1024
        ),
    )(compressed, maps, mask, *tables())


def solution(mesh):
    placed = (
        P(None, None, "slab", "coil", None),
        P(None, "slab", None, None),
        P(None, "coil", None, "slab", None),
        P(),
    )
    return jax.shard_map(
        shards,
        mesh=mesh,
        in_specs=placed,
        out_specs=(P(None, None, "slab", None), P(None, None, "slab", None)),
        check_vma=False,
    )
```

```python
import math

import jax
import jax.numpy as jnp
import ml_dtypes
import numpy as np
from jax import lax
from jax.experimental import pallas as pl
from jax.experimental.pallas import tpu as pltpu
from jax.sharding import PartitionSpec as P

MESH = pl.DeviceIdType.MESH
BF16 = jnp.bfloat16
F32 = jnp.float32

RIDGE = 0.5
SLABS = 64
GROUPS = 4
COILS = 4
ROWS = 512
DEPTH = 256
CHUNKS = 4
CHUNK = ROWS // CHUNKS
SLICE = 16
SLICES = ROWS // GROUPS // SLICE
BLOCKS = SLABS // CHUNKS


def place(slab):
    z, x, core = lax.div(slab, 8), lax.rem(lax.div(slab, 2), 4), lax.rem(slab, 2)
    return lax.rem(z + x, 2) * 2 + core, z * 2 + lax.div(x, 2)


def member(chunk, index):
    z = lax.div(index, 2)
    x = 2 * lax.rem(index, 2) + lax.rem(z + lax.div(chunk, 2), 2)
    return z * 8 + x * 2 + lax.rem(chunk, 2)


def tables():
    def cos_sin(length):
        index = np.arange(length, dtype=np.int64)
        angle = (index[:, None] * index[None, :] % length) * (2.0 * math.pi / length)
        return np.cos(angle) / math.sqrt(length), np.sin(angle) / math.sqrt(length)

    slab = np.arange(SLABS)
    z, x, core = slab // 8, slab // 2 % 4, slab % 2
    position = ((z + x) % 2 * 2 + core) * BLOCKS + z * 2 + x // 2
    order = np.zeros(SLABS, np.int64)
    order[position] = slab
    rows = (order[:, None] * 8 + np.arange(8)[None, :]).reshape(-1)
    cosine, sine = cos_sin(ROWS)
    cosine, sine = cosine[:, rows], sine[:, rows]
    rows_forward = np.block([[cosine, sine], [-sine, cosine]])
    rows_inverse = np.block([[cosine.T, -sine.T], [sine.T, cosine.T]])
    rows_inverse = rows_inverse.reshape(2, CHUNKS, CHUNK, 2 * ROWS).swapaxes(0, 1).reshape(2 * ROWS, 2 * ROWS)
    cosine, sine = cos_sin(DEPTH)
    depth_forward = np.block([[cosine, -sine], [sine, cosine]])
    depth_inverse = np.block([[cosine, sine], [-sine, cosine]])
    return [
        jnp.asarray(table.astype(ml_dtypes.bfloat16))
        for table in (rows_forward, rows_inverse, depth_forward, depth_inverse)
    ]


def dot(left, right):
    return jnp.dot(left, right, preferred_element_type=F32)


def kernel(
    gcc, raw_hbm, sens_hbm, mask_hbm, rf_hbm, ri_hbm, df_hbm, di_hbm,
    sol_ref, res_ref,
    raw, mix, comp, whole_mask, acc,
    kd, sb, mask, rf, ri, df, di,
    zbuf, mbuf, early, lhs,
    part, got1, sum1, got2, cs, rowbuf,
    ysc, zsc, tile,
    raw_sem, load_sem, kd_send, kd_recv, sb_send, sb_recv,
    p1_send, p1_recv, p2_send, p2_recv, p3_send, p3_recv,
    rb_send, rb_recv, last_send, last_recv, ys_send, ys_recv, zs_send, zs_recv,
):
    me = lax.axis_index("slab")
    group = lax.axis_index("coil")
    my_chunk, my_index = place(me)
    my_place = my_chunk * BLOCKS + my_index
    side_a = group + 1 - 2 * lax.rem(group, 2)
    side_b = 3 - group
    half_a = lax.rem(lax.div(group + 1, 2), 2)
    half_b = lax.div(group, 2)

    barrier = pltpu.get_barrier_semaphore()

    def greet(step, carry):
        peer = lax.rem(me + step, SLABS)
        pl.semaphore_signal(barrier, inc=1, device_id=(peer, group), device_id_type=MESH)
        return carry

    lax.fori_loop(1, SLABS, greet, 0)
    for step in range(1, GROUPS):
        pl.semaphore_signal(
            barrier, inc=1, device_id=(me, lax.rem(group + step, GROUPS)), device_id_type=MESH
        )

    maps_load = pltpu.make_async_copy(sens_hbm.at[:, me], sb.at[:, my_place], load_sem.at[0])
    mask_load = pltpu.make_async_copy(mask_hbm, whole_mask, load_sem.at[1])
    rows_load = pltpu.make_async_copy(ri_hbm, ri, load_sem.at[2])
    late_loads = [
        maps_load,
        pltpu.make_async_copy(di_hbm, di, load_sem.at[3]),
        pltpu.make_async_copy(df_hbm, df, load_sem.at[4]),
        pltpu.make_async_copy(rf_hbm, rf, load_sem.at[5]),
    ]

    def raw_load(step):
        return pltpu.make_async_copy(
            raw_hbm.at[:, pl.ds(step * SLICE, SLICE), :], raw.at[step], raw_sem.at[step]
        )

    def start_raw(step, carry):
        raw_load(step).start()
        return carry

    lax.fori_loop(0, SLICES, start_raw, 0)
    for load in [mask_load, rows_load] + late_loads:
        load.start()

    pl.semaphore_wait(barrier, SLABS - 1 + GROUPS - 1)

    def settle(ref, sem):
        pltpu.make_async_copy(ref, ref, sem).wait()

    def send_maps(phase):
        chunk = lax.rem(my_chunk + phase, CHUNKS)

        def send(step, carry):
            peer = member(chunk, lax.rem(my_index + 5 * step, BLOCKS))
            pltpu.make_async_remote_copy(
                src_ref=sens_hbm.at[:, peer], dst_ref=sb.at[:, my_place],
                send_sem=sb_send.at[phase], recv_sem=sb_recv.at[my_chunk],
                device_id=(peer, group), device_id_type=MESH,
            ).start()
            return carry

        lax.fori_loop(0 if phase else 1, BLOCKS, send, 0)

    def maps_left(phase):
        settle(sb.at[:, pl.ds(0, BLOCKS if phase else BLOCKS - 1)], sb_send.at[phase])

    send_maps(0)
    send_maps(1)

    def turn_order(step):
        return lax.rem(my_chunk + CHUNKS - step, CHUNKS)

    def same(shape, left, right):
        one = lax.broadcasted_iota(jnp.int32, shape, 0)
        two = lax.broadcasted_iota(jnp.int32, shape, 1)
        return left(one) == right(two)

    up = same((16 * SLICE, 16), lambda a: a // SLICE, lambda b: b).astype(F32).astype(BF16)
    across = same((64, 64 * SLICE), lambda a: a, lambda b: b // SLICE).astype(F32).astype(BF16)
    diagonal = same((16 * SLICE, 64 * SLICE), lambda a: a % SLICE, lambda b: b % SLICE)
    real, imag = [
        jnp.where(diagonal, dot(dot(up, gcc[index]).astype(BF16), across), 0.0) for index in range(2)
    ]
    tall, wide = 16 * SLICE, 64 * SLICE
    mix[:tall, :wide] = real.astype(BF16)
    mix[:tall, wide:] = (-imag).astype(BF16)
    mix[tall:, :wide] = imag.astype(BF16)
    mix[tall:, wide:] = real.astype(BF16)

    def compress(step, carry):
        raw_load(step).wait()
        out = dot(mix[...], raw[step].reshape(2 * wide, DEPTH))
        here = pl.ds(step * SLICE, SLICE)
        there = pl.ds(CHUNK * group + step * SLICE, SLICE)
        comp[:, :, here, :] = out.astype(BF16).reshape(2, 16, SLICE, DEPTH)
        kd[:, :, there, :] = comp[:, pl.ds(COILS * group, COILS), here, :]
        for shift in range(1, GROUPS):
            peer = lax.rem(group + shift, GROUPS)
            pltpu.make_async_remote_copy(
                src_ref=comp.at[:, pl.ds(COILS * peer, COILS), here, :],
                dst_ref=kd.at[:, :, there, :],
                send_sem=kd_send, recv_sem=kd_recv,
                device_id=(me, peer), device_id_type=MESH,
            ).start()
        return carry

    lax.fori_loop(0, SLICES, compress, 0)
    for phase in range(2):
        maps_left(phase)
        send_maps(phase + 2)
    mask_load.wait()
    mask[...] = whole_mask[...].astype(F32).astype(BF16)
    rows_load.wait()
    settle(kd.at[:, :, pl.ds(0, CHUNK * 3), :], kd_recv)

    def inverse(chunk):
        def coil_rows(coil, carry):
            out = dot(ri[pl.ds(chunk * 2 * CHUNK, 2 * CHUNK), :], mbuf[coil]).astype(BF16)
            rows = pl.ds(pl.multiple_of(coil * CHUNK, CHUNK), CHUNK)
            lhs[rows, :DEPTH] = out[:CHUNK]
            lhs[rows, DEPTH:] = out[CHUNK:]
            return carry

        lax.fori_loop(0, COILS, coil_rows, 0, unroll=True)
        return dot(lhs[...], di[...])

    for load in late_loads:
        load.wait()

    def data_coil(coil, carry):
        for half in range(2):
            mbuf[coil, half * ROWS:(half + 1) * ROWS, :] = kd[half, coil] * mask[...]
        return carry

    lax.fori_loop(0, COILS, data_coil, 0)

    def data_chunk(chunk, carry):
        early[chunk] = inverse(chunk)
        return carry

    lax.fori_loop(0, CHUNKS, data_chunk, 0)

    def maps_of(coil, chunk):
        both = sb[coil, pl.ds(chunk * BLOCKS, BLOCKS)].astype(F32)
        return both[:, :8].reshape(CHUNK, DEPTH), both[:, 8:].reshape(CHUNK, DEPTH)

    def route(chunk):
        odd = lax.rem(chunk, 2)
        first = side_a + odd * (side_b - side_a)
        second = side_b + odd * (side_a - side_b)
        return first, second, half_a + odd * (half_b - half_a)

    def columns(half):
        return pl.ds(pl.multiple_of(half * 128, 128), 128)

    def blocks(chunk):
        return pl.ds(chunk * BLOCKS, BLOCKS)

    def combine(turn, chunk):
        out = early[chunk] if turn == 0 else inverse(chunk)
        real = imag = None
        for coil in range(COILS):
            a = out[coil * CHUNK:(coil + 1) * CHUNK, :DEPTH]
            b = out[coil * CHUNK:(coil + 1) * CHUNK, DEPTH:]
            sr, si = maps_of(coil, chunk)
            re, im = sr * a + si * b, sr * b - si * a
            real = re if real is None else real + re
            imag = im if imag is None else imag + im
        packed = jnp.concatenate(
            [real.reshape(BLOCKS, 8, DEPTH), imag.reshape(BLOCKS, 8, DEPTH)], axis=1
        )
        part[turn, blocks(chunk)] = packed.astype(BF16)
        first, second, half = route(chunk)
        pltpu.make_async_remote_copy(
            src_ref=part.at[turn, blocks(chunk), :, columns(1 - half)],
            dst_ref=got1.at[turn, chunk],
            send_sem=p1_send.at[turn], recv_sem=p1_recv.at[turn, chunk],
            device_id=(me, first), device_id_type=MESH,
        ).start()

    def second_step(turn, chunk):
        first, second, half = route(chunk)
        settle(got1.at[turn, chunk], p1_recv.at[turn, chunk])
        mine = part[turn, blocks(chunk), :, columns(half)].astype(F32)
        sum1[turn, chunk] = (mine + got1[turn, chunk].astype(F32)).astype(BF16)
        pltpu.make_async_remote_copy(
            src_ref=sum1.at[turn, chunk], dst_ref=got2.at[turn, chunk],
            send_sem=p2_send.at[turn], recv_sem=p2_recv.at[turn, chunk],
            device_id=(me, second), device_id_type=MESH,
        ).start()

    def third_step(turn, chunk):
        first, second, half = route(chunk)
        settle(got2.at[turn, chunk], p2_recv.at[turn, chunk])
        whole = sum1[turn, chunk].astype(F32) + got2[turn, chunk].astype(F32)
        cs[turn, blocks(chunk), :, columns(half)] = whole.astype(BF16)
        if turn == 2:
            send_rows(turn, chunk, columns(half))
            return
        pltpu.make_async_remote_copy(
            src_ref=cs.at[turn, blocks(chunk), :, columns(half)],
            dst_ref=cs.at[turn, blocks(chunk), :, columns(half)],
            send_sem=p3_send.at[turn], recv_sem=p3_recv.at[turn, chunk],
            device_id=(me, first), device_id_type=MESH,
        ).start()

    def over_chunks(work, turn):
        def step(index, carry):
            work(turn, turn_order(index))
            return carry

        lax.fori_loop(0, CHUNKS, step, 0)

    def receive_chunk(turn, chunk):
        first, second, half = route(chunk)
        settle(cs.at[turn, blocks(chunk), :, columns(1 - half)], p3_recv.at[turn, chunk])

    def send_rows(turn, chunk, lanes=slice(None)):
        def send(step, carry):
            to = lax.rem(my_index + step, BLOCKS)
            peer = member(chunk, to)

            @pl.when(peer != me)
            def _():
                pltpu.make_async_remote_copy(
                    src_ref=cs.at[turn, chunk * BLOCKS + to, :, lanes],
                    dst_ref=rowbuf.at[turn, me, :, lanes],
                    send_sem=rb_send.at[turn], recv_sem=rb_recv.at[turn],
                    device_id=(peer, group), device_id_type=MESH,
                ).start()

            return carry

        lax.fori_loop(0, BLOCKS, send, 0)

    def image(turn, chunk):
        both = cs[turn, pl.ds(chunk * BLOCKS, BLOCKS)].astype(F32)
        return both[:, :8].reshape(CHUNK, DEPTH), both[:, 8:].reshape(CHUNK, DEPTH)

    def fold_rows(values):
        return jnp.sum(values.reshape(-1, 8, DEPTH), axis=0)

    def total(values):
        return jnp.sum(values, keepdims=True)

    def spread_groups(turn, value):
        ysc[turn, group] = jnp.broadcast_to(value, (8, 128))
        for step in range(1, GROUPS):
            peer = lax.rem(group + step, GROUPS)
            pltpu.make_async_remote_copy(
                src_ref=ysc.at[turn, group], dst_ref=ysc.at[turn, group],
                send_sem=ys_send.at[turn], recv_sem=ys_recv.at[turn],
                device_id=(me, peer), device_id_type=MESH,
            ).start()

    def spread_slabs(turn, values):
        settle(ysc.at[turn, pl.ds(0, GROUPS - 1)], ys_recv.at[turn])
        spectral = jnp.sum(ysc[turn], axis=0)
        row = lax.broadcasted_iota(jnp.int32, (8, 128), 0)
        for index, value in enumerate(values):
            spectral = jnp.where(row == index + 1, jnp.broadcast_to(value, (8, 128)), spectral)
        tile[turn] = spectral
        zsc[turn, me] = spectral

        def send(step, carry):
            peer = lax.rem(me + step, SLABS)
            pltpu.make_async_remote_copy(
                src_ref=tile.at[turn], dst_ref=zsc.at[turn, me],
                send_sem=zs_send.at[turn], recv_sem=zs_recv.at[turn],
                device_id=(peer, group), device_id_type=MESH,
            ).start()
            return carry

        lax.fori_loop(1, SLABS, send, 0)

    def collect(turn):
        settle(zsc.at[turn, pl.ds(0, SLABS - 1)], zs_recv.at[turn])
        summed = jnp.sum(zsc[turn], axis=0)
        return [summed[index:index + 1, 0:1] for index in range(3)]

    def front(turn, chunk):
        receive_chunk(turn, chunk)
        pr, pi = image(0, chunk)
        if turn == 1:
            ar, ai = image(1, chunk)
            ar, ai = ar + RIDGE * pr, ai + RIDGE * pi
            pr, pi = pr - alpha * ar, pi - alpha * ai
            acc[turn, 1] += fold_rows(pr * ar + pi * ai)
        acc[turn, 0] += fold_rows(pr * pr + pi * pi)
        for coil in range(COILS):
            sr, si = maps_of(coil, chunk)
            rows = pl.ds(coil * CHUNK, CHUNK)
            lhs[rows, :DEPTH] = (sr * pr - si * pi).astype(BF16)
            lhs[rows, DEPTH:] = (sr * pi + si * pr).astype(BF16)
        out = dot(lhs[...], df[...])
        for coil in range(COILS):
            rows = slice(coil * CHUNK, (coil + 1) * CHUNK)
            zbuf[coil, pl.ds(chunk * CHUNK, CHUNK), :] = out[rows, :DEPTH].astype(BF16)
            zbuf[coil, pl.ds(ROWS + chunk * CHUNK, CHUNK), :] = out[rows, DEPTH:].astype(BF16)

    zero = jnp.zeros((8, DEPTH), F32)
    acc[...] = jnp.zeros_like(acc)

    def arrivals(step, carry):
        @pl.when(step == 0)
        def _():
            settle(sb.at[:, pl.ds(0, BLOCKS - 1)], sb_recv.at[my_chunk])

        @pl.when((step > 0) & (step < CHUNKS))
        def _():
            settle(sb.at[:, pl.ds(0, BLOCKS)], sb_recv.at[turn_order(step)])

        @pl.when(step < CHUNKS)
        def _():
            combine(0, turn_order(step))

        @pl.when((step >= 1) & (step < CHUNKS + 1))
        def _():
            second_step(0, turn_order(step - 1))

        @pl.when((step >= 2) & (step < CHUNKS + 2))
        def _():
            third_step(0, turn_order(step - 2))

        @pl.when(step >= 3)
        def _():
            front(0, turn_order(step - 3))

        return carry

    lax.fori_loop(0, CHUNKS + 3, arrivals, 0)

    alpha = None
    for turn in range(2):
        if turn == 1:
            over_chunks(front, 1)

        def rows_coil(coil, energy):
            send_rows(turn, turn_order(coil))
            for half in range(2):
                out = dot(rf[half * ROWS:(half + 1) * ROWS, :], zbuf[coil])
                weighted = out.astype(BF16) * mask[...]
                mbuf[coil, half * ROWS:(half + 1) * ROWS, :] = weighted
                wide = weighted.astype(F32)
                energy = energy + fold_rows(wide * wide)
            return energy

        energy = lax.fori_loop(0, COILS, rows_coil, zero)
        spread_groups(turn, total(energy))
        over_chunks(combine, turn + 1)
        spread_slabs(turn, (total(acc[turn, 0]), total(acc[turn, 1])))
        over_chunks(second_step, turn + 1)
        over_chunks(third_step, turn + 1)
        if turn == 0:
            spectral, norm0, _ = collect(0)
            energy0 = spectral + RIDGE * norm0
            alpha = norm0 / energy0

    for turn in range(2):
        rowbuf[turn, me] = cs[turn, my_place]
        settle(rowbuf.at[turn, pl.ds(0, SLABS - 1)], rb_recv.at[turn])
    first, second, half = route(my_chunk)
    rowbuf[2, me, :, columns(half)] = cs[2, my_place, :, columns(half)]
    settle(rowbuf.at[2, pl.ds(0, SLABS - 1), :, columns(half)], rb_recv.at[2])

    def swap(step, carry):
        some = pl.ds(step * 16, 16)
        pltpu.make_async_remote_copy(
            src_ref=rowbuf.at[2, some, :, columns(half)], dst_ref=rowbuf.at[2, some, :, columns(half)],
            send_sem=last_send, recv_sem=last_recv.at[step],
            device_id=(me, first), device_id_type=MESH,
        ).start()
        return carry

    lax.fori_loop(0, SLABS // 16, swap, 0)
    spectral, norm1, cross1 = collect(1)
    beta = norm1 / norm0
    energy1 = spectral + RIDGE * norm1 + 2.0 * beta * cross1 + beta * beta * energy0
    alpha1 = norm1 / energy1
    def finish(step, carry):
        some = pl.ds(step * 16, 16)
        settle(rowbuf.at[2, some, :, columns(1 - half)], last_recv.at[step])
        start = rowbuf[0, some].astype(F32)
        applied = rowbuf[1, some].astype(F32) + RIDGE * start
        residual = start - alpha * applied
        again = rowbuf[2, some].astype(F32) + RIDGE * residual
        direction = residual + beta * start
        answer = alpha * start + alpha1 * direction
        left = residual - alpha1 * (again + beta * applied)
        for index in range(2):
            sol_ref[index, some] = answer[:, index * 8:index * 8 + 8]
            res_ref[index, some] = left[:, index * 8:index * 8 + 8]
        return carry

    lax.fori_loop(0, SLABS // 16, finish, 0)

    settle(kd.at[:, :, pl.ds(0, CHUNK * 3), :], kd_send)
    for phase in range(2, CHUNKS):
        maps_left(phase)
    for turn in range(3):
        settle(got1.at[turn], p1_send.at[turn])
        settle(got1.at[turn], p2_send.at[turn])
    for turn in range(2):
        settle(got1.at[turn], p3_send.at[turn])
        settle(rowbuf.at[turn, pl.ds(0, SLABS - 1)], rb_send.at[turn])
    settle(rowbuf.at[2, pl.ds(0, SLABS - 1), :, columns(half)], rb_send.at[2])
    settle(rowbuf.at[2, :, :, columns(half)], last_send)
    for turn in range(2):
        settle(ysc.at[turn, pl.ds(0, GROUPS - 1)], ys_send.at[turn])
        settle(zsc.at[turn, pl.ds(0, SLABS - 1)], zs_send.at[turn])


def shards(raw_data, gcc_matrix, sens_maps, line_mask):
    gcc = gcc_matrix.reshape(2, 16, 64)
    raw = raw_data.reshape(2 * 64, ROWS // GROUPS, DEPTH)
    maps = jnp.transpose(sens_maps, (1, 2, 0, 3, 4)).reshape(COILS, SLABS, 16, DEPTH)

    dma = pltpu.SemaphoreType.DMA
    out = jax.ShapeDtypeStruct((2, SLABS, 8, DEPTH), F32)
    return pl.pallas_call(
        kernel,
        out_shape=(out, out),
        in_specs=[pl.BlockSpec(memory_space=pltpu.VMEM)] + [pl.BlockSpec(memory_space=pl.ANY)] * 7,
        out_specs=(pl.BlockSpec(memory_space=pltpu.VMEM),) * 2,
        scratch_shapes=[
            pltpu.VMEM((SLICES, 2 * 64, SLICE, DEPTH), BF16),
            pltpu.VMEM((2 * 16 * SLICE, 2 * 64 * SLICE), BF16),
            pltpu.VMEM((2, 16, ROWS // GROUPS, DEPTH), BF16),
            pltpu.VMEM((ROWS, DEPTH), jnp.int32),
            pltpu.VMEM((2, 2, 8, DEPTH), F32),
            pltpu.VMEM((2, COILS, ROWS, DEPTH), BF16),
            pltpu.VMEM((COILS, SLABS, 16, DEPTH), BF16),
            pltpu.VMEM((ROWS, DEPTH), BF16),
            pltpu.VMEM((2 * ROWS, 2 * ROWS), BF16),
            pltpu.VMEM((2 * ROWS, 2 * ROWS), BF16),
            pltpu.VMEM((2 * DEPTH, 2 * DEPTH), BF16),
            pltpu.VMEM((2 * DEPTH, 2 * DEPTH), BF16),
            pltpu.VMEM((COILS, 2 * ROWS, DEPTH), BF16),
            pltpu.VMEM((COILS, 2 * ROWS, DEPTH), BF16),
            pltpu.VMEM((CHUNKS, COILS * CHUNK, 2 * DEPTH), F32),
            pltpu.VMEM((COILS * CHUNK, 2 * DEPTH), BF16),
            pltpu.VMEM((3, SLABS, 16, DEPTH), BF16),
            pltpu.VMEM((3, CHUNKS, BLOCKS, 16, 128), BF16),
            pltpu.VMEM((3, CHUNKS, BLOCKS, 16, 128), BF16),
            pltpu.VMEM((3, CHUNKS, BLOCKS, 16, 128), BF16),
            pltpu.VMEM((3, SLABS, 16, DEPTH), BF16),
            pltpu.VMEM((3, SLABS, 16, DEPTH), BF16),
            pltpu.VMEM((2, GROUPS, 8, 128), F32),
            pltpu.VMEM((2, SLABS, 8, 128), F32),
            pltpu.VMEM((2, 8, 128), F32),
            dma((SLICES,)), dma((6,)), dma, dma, dma((CHUNKS,)), dma((CHUNKS,)),
            dma((3,)), dma((3, CHUNKS)), dma((3,)), dma((3, CHUNKS)), dma((2,)), dma((2, CHUNKS)),
            dma((3,)), dma((3,)), dma, dma((SLABS // 16,)), dma((2,)), dma((2,)), dma((2,)), dma((2,)),
        ],
        compiler_params=pltpu.CompilerParams(
            collective_id=0, has_side_effects=True, vmem_limit_bytes=48 * 1024 * 1024
        ),
    )(gcc, raw, maps, line_mask, *tables())


def solution(mesh):
    placed = (
        P(None, None, "slab", "coil", None),
        P(None, "slab", None, None),
        P(None, "coil", None, "slab", None),
        P(),
    )
    return jax.shard_map(
        shards,
        mesh=mesh,
        in_specs=placed,
        out_specs=(P(None, None, "slab", None), P(None, None, "slab", None)),
        check_vma=False,
    )
```

```python
import math

import jax
import jax.numpy as jnp
import ml_dtypes
import numpy as np
from jax import lax
from jax.experimental import pallas as pl
from jax.experimental.pallas import tpu as pltpu
from jax.sharding import PartitionSpec as P

MESH = pl.DeviceIdType.MESH
BF16 = jnp.bfloat16
F32 = jnp.float32

RIDGE = 0.5
SLABS = 64
GROUPS = 4
COILS = 4
ROWS = 512
DEPTH = 256
CHUNKS = 4
CHUNK = ROWS // CHUNKS
SLICE = 16
SLICES = ROWS // GROUPS // SLICE
BLOCKS = SLABS // CHUNKS


def place(slab):
    z, x, core = lax.div(slab, 8), lax.rem(lax.div(slab, 2), 4), lax.rem(slab, 2)
    return lax.rem(z + x, 2) * 2 + core, z * 2 + lax.div(x, 2)


def member(chunk, index):
    z = lax.div(index, 2)
    x = 2 * lax.rem(index, 2) + lax.rem(z + lax.div(chunk, 2), 2)
    return z * 8 + x * 2 + lax.rem(chunk, 2)


def tables():
    def cos_sin(length):
        index = np.arange(length, dtype=np.int64)
        angle = (index[:, None] * index[None, :] % length) * (2.0 * math.pi / length)
        return np.cos(angle) / math.sqrt(length), np.sin(angle) / math.sqrt(length)

    slab = np.arange(SLABS)
    z, x, core = slab // 8, slab // 2 % 4, slab % 2
    position = ((z + x) % 2 * 2 + core) * BLOCKS + z * 2 + x // 2
    order = np.zeros(SLABS, np.int64)
    order[position] = slab
    rows = (order[:, None] * 8 + np.arange(8)[None, :]).reshape(-1)
    cosine, sine = cos_sin(ROWS)
    cosine, sine = cosine[:, rows], sine[:, rows]
    rows_forward = np.block([[cosine, sine], [-sine, cosine]])
    rows_inverse = np.block([[cosine.T, -sine.T], [sine.T, cosine.T]])
    rows_inverse = rows_inverse.reshape(2, CHUNKS, CHUNK, 2 * ROWS).swapaxes(0, 1).reshape(2 * ROWS, 2 * ROWS)
    cosine, sine = cos_sin(DEPTH)
    depth_forward = np.block([[cosine, -sine], [sine, cosine]])
    depth_inverse = np.block([[cosine, sine], [-sine, cosine]])
    return [
        jnp.asarray(table.astype(ml_dtypes.bfloat16))
        for table in (rows_forward, rows_inverse, depth_forward, depth_inverse)
    ]


def dot(left, right):
    return jnp.dot(left, right, preferred_element_type=F32)


def kernel(
    gcc, raw_hbm, sens_hbm, mask_hbm, rf_hbm, ri_hbm, df_hbm, di_hbm,
    sol_ref, res_ref,
    raw, mix, comp, whole_mask, acc,
    kd, sb, mask, rf, ri, df, di,
    zbuf, mbuf, early, lhs,
    part, got1, sum1, got2, cs, rowbuf,
    ysc, zsc, tile,
    raw_sem, load_sem, kd_send, kd_recv, sb_send, sb_recv,
    p1_send, p1_recv, p2_send, p2_recv, p3_send, p3_recv,
    rb_send, rb_recv, last_send, last_recv, ys_send, ys_recv, zs_send, zs_recv,
):
    me = lax.axis_index("slab")
    group = lax.axis_index("coil")
    my_chunk, my_index = place(me)
    my_place = my_chunk * BLOCKS + my_index
    side_a = group + 1 - 2 * lax.rem(group, 2)
    side_b = 3 - group
    half_a = lax.rem(lax.div(group + 1, 2), 2)
    half_b = lax.div(group, 2)

    barrier = pltpu.get_barrier_semaphore()

    def greet(step, carry):
        peer = lax.rem(me + step, SLABS)
        pl.semaphore_signal(barrier, inc=1, device_id=(peer, group), device_id_type=MESH)
        return carry

    lax.fori_loop(1, SLABS, greet, 0)
    for step in range(1, GROUPS):
        pl.semaphore_signal(
            barrier, inc=1, device_id=(me, lax.rem(group + step, GROUPS)), device_id_type=MESH
        )

    maps_load = pltpu.make_async_copy(sens_hbm.at[:, me], sb.at[:, my_place], load_sem.at[0])
    mask_load = pltpu.make_async_copy(mask_hbm, whole_mask, load_sem.at[1])
    rows_load = pltpu.make_async_copy(ri_hbm, ri, load_sem.at[2])
    late_loads = [
        maps_load,
        pltpu.make_async_copy(di_hbm, di, load_sem.at[3]),
        pltpu.make_async_copy(df_hbm, df, load_sem.at[4]),
        pltpu.make_async_copy(rf_hbm, rf, load_sem.at[5]),
    ]

    def raw_load(step):
        return pltpu.make_async_copy(
            raw_hbm.at[:, pl.ds(step * SLICE, SLICE), :], raw.at[step], raw_sem.at[step]
        )

    def start_raw(step, carry):
        raw_load(step).start()
        return carry

    lax.fori_loop(0, SLICES, start_raw, 0)
    for load in [mask_load, rows_load] + late_loads:
        load.start()

    pl.semaphore_wait(barrier, SLABS - 1 + GROUPS - 1)

    def settle(ref, sem):
        pltpu.make_async_copy(ref, ref, sem).wait()

    def send_maps(phase):
        chunk = lax.rem(my_chunk + phase, CHUNKS)

        def send(step, carry):
            peer = member(chunk, lax.rem(my_index + 5 * step, BLOCKS))
            pltpu.make_async_remote_copy(
                src_ref=sens_hbm.at[:, peer], dst_ref=sb.at[:, my_place],
                send_sem=sb_send.at[phase], recv_sem=sb_recv.at[my_chunk],
                device_id=(peer, group), device_id_type=MESH,
            ).start()
            return carry

        lax.fori_loop(0 if phase else 1, BLOCKS, send, 0)

    def maps_left(phase):
        settle(sb.at[:, pl.ds(0, BLOCKS if phase else BLOCKS - 1)], sb_send.at[phase])

    send_maps(0)
    send_maps(1)

    def turn_order(step):
        return lax.rem(my_chunk + CHUNKS - step, CHUNKS)

    def same(shape, left, right):
        one = lax.broadcasted_iota(jnp.int32, shape, 0)
        two = lax.broadcasted_iota(jnp.int32, shape, 1)
        return left(one) == right(two)

    up = same((16 * SLICE, 16), lambda a: a // SLICE, lambda b: b).astype(F32).astype(BF16)
    across = same((64, 64 * SLICE), lambda a: a, lambda b: b // SLICE).astype(F32).astype(BF16)
    diagonal = same((16 * SLICE, 64 * SLICE), lambda a: a % SLICE, lambda b: b % SLICE)
    real, imag = [
        jnp.where(diagonal, dot(dot(up, gcc[index]).astype(BF16), across), 0.0) for index in range(2)
    ]
    tall, wide = 16 * SLICE, 64 * SLICE
    mix[:tall, :wide] = real.astype(BF16)
    mix[:tall, wide:] = (-imag).astype(BF16)
    mix[tall:, :wide] = imag.astype(BF16)
    mix[tall:, wide:] = real.astype(BF16)

    def compress(step, carry):
        raw_load(step).wait()
        out = dot(mix[...], raw[step].reshape(2 * wide, DEPTH))
        here = pl.ds(step * SLICE, SLICE)
        there = pl.ds(CHUNK * group + step * SLICE, SLICE)
        comp[:, :, here, :] = out.astype(BF16).reshape(2, 16, SLICE, DEPTH)
        kd[:, :, there, :] = comp[:, pl.ds(COILS * group, COILS), here, :]
        for shift in range(1, GROUPS):
            peer = lax.rem(group + shift, GROUPS)
            pltpu.make_async_remote_copy(
                src_ref=comp.at[:, pl.ds(COILS * peer, COILS), here, :],
                dst_ref=kd.at[:, :, there, :],
                send_sem=kd_send, recv_sem=kd_recv,
                device_id=(me, peer), device_id_type=MESH,
            ).start()
        return carry

    lax.fori_loop(0, SLICES, compress, 0)
    for phase in range(2):
        maps_left(phase)
        send_maps(phase + 2)
    mask_load.wait()
    mask[...] = whole_mask[...].astype(F32).astype(BF16)
    rows_load.wait()
    settle(kd.at[:, :, pl.ds(0, CHUNK * 3), :], kd_recv)

    def inverse(chunk):
        def coil_rows(coil, carry):
            out = dot(ri[pl.ds(chunk * 2 * CHUNK, 2 * CHUNK), :], mbuf[coil]).astype(BF16)
            rows = pl.ds(pl.multiple_of(coil * CHUNK, CHUNK), CHUNK)
            lhs[rows, :DEPTH] = out[:CHUNK]
            lhs[rows, DEPTH:] = out[CHUNK:]
            return carry

        lax.fori_loop(0, COILS, coil_rows, 0, unroll=True)
        return dot(lhs[...], di[...])

    for load in late_loads:
        load.wait()

    def data_coil(coil, carry):
        for half in range(2):
            mbuf[coil, half * ROWS:(half + 1) * ROWS, :] = kd[half, coil] * mask[...]
        return carry

    lax.fori_loop(0, COILS, data_coil, 0)

    def data_chunk(chunk, carry):
        early[chunk] = inverse(chunk)
        return carry

    lax.fori_loop(0, CHUNKS, data_chunk, 0)

    def maps_of(coil, chunk):
        both = sb[coil, pl.ds(chunk * BLOCKS, BLOCKS)].astype(F32)
        return both[:, :8].reshape(CHUNK, DEPTH), both[:, 8:].reshape(CHUNK, DEPTH)

    def route(chunk):
        odd = lax.rem(chunk, 2)
        first = side_a + odd * (side_b - side_a)
        second = side_b + odd * (side_a - side_b)
        return first, second, half_a + odd * (half_b - half_a)

    def columns(half):
        return pl.ds(pl.multiple_of(half * 128, 128), 128)

    def blocks(chunk):
        return pl.ds(chunk * BLOCKS, BLOCKS)

    def combine(turn, chunk):
        out = early[chunk] if turn == 0 else inverse(chunk)
        real = imag = None
        for coil in range(COILS):
            a = out[coil * CHUNK:(coil + 1) * CHUNK, :DEPTH]
            b = out[coil * CHUNK:(coil + 1) * CHUNK, DEPTH:]
            sr, si = maps_of(coil, chunk)
            re, im = sr * a + si * b, sr * b - si * a
            real = re if real is None else real + re
            imag = im if imag is None else imag + im
        packed = jnp.concatenate(
            [real.reshape(BLOCKS, 8, DEPTH), imag.reshape(BLOCKS, 8, DEPTH)], axis=1
        )
        part[turn, blocks(chunk)] = packed.astype(BF16)
        first, second, half = route(chunk)
        pltpu.make_async_remote_copy(
            src_ref=part.at[turn, blocks(chunk), :, columns(1 - half)],
            dst_ref=got1.at[turn, chunk],
            send_sem=p1_send.at[turn], recv_sem=p1_recv.at[turn, chunk],
            device_id=(me, first), device_id_type=MESH,
        ).start()

    def second_step(turn, chunk):
        first, second, half = route(chunk)
        settle(got1.at[turn, chunk], p1_recv.at[turn, chunk])
        mine = part[turn, blocks(chunk), :, columns(half)].astype(F32)
        sum1[turn, chunk] = (mine + got1[turn, chunk].astype(F32)).astype(BF16)
        pltpu.make_async_remote_copy(
            src_ref=sum1.at[turn, chunk], dst_ref=got2.at[turn, chunk],
            send_sem=p2_send.at[turn], recv_sem=p2_recv.at[turn, chunk],
            device_id=(me, second), device_id_type=MESH,
        ).start()

    def third_step(turn, chunk):
        first, second, half = route(chunk)
        settle(got2.at[turn, chunk], p2_recv.at[turn, chunk])
        whole = sum1[turn, chunk].astype(F32) + got2[turn, chunk].astype(F32)
        cs[turn, blocks(chunk), :, columns(half)] = whole.astype(BF16)
        if turn == 2:
            send_rows(turn, chunk, columns(half))
            return
        pltpu.make_async_remote_copy(
            src_ref=cs.at[turn, blocks(chunk), :, columns(half)],
            dst_ref=cs.at[turn, blocks(chunk), :, columns(half)],
            send_sem=p3_send.at[turn], recv_sem=p3_recv.at[turn, chunk],
            device_id=(me, first), device_id_type=MESH,
        ).start()

    def over_chunks(work, turn):
        def step(index, carry):
            work(turn, turn_order(index))
            return carry

        lax.fori_loop(0, CHUNKS, step, 0)

    def receive_chunk(turn, chunk):
        first, second, half = route(chunk)
        settle(cs.at[turn, blocks(chunk), :, columns(1 - half)], p3_recv.at[turn, chunk])

    def send_rows(turn, chunk, lanes=slice(None)):
        def send(step, carry):
            to = lax.rem(my_index + step, BLOCKS)
            peer = member(chunk, to)

            @pl.when(peer != me)
            def _():
                pltpu.make_async_remote_copy(
                    src_ref=cs.at[turn, chunk * BLOCKS + to, :, lanes],
                    dst_ref=rowbuf.at[turn, me, :, lanes],
                    send_sem=rb_send.at[turn], recv_sem=rb_recv.at[turn],
                    device_id=(peer, group), device_id_type=MESH,
                ).start()

            return carry

        lax.fori_loop(0, BLOCKS, send, 0)

    def image(turn, chunk):
        both = cs[turn, pl.ds(chunk * BLOCKS, BLOCKS)].astype(F32)
        return both[:, :8].reshape(CHUNK, DEPTH), both[:, 8:].reshape(CHUNK, DEPTH)

    def fold_rows(values):
        return jnp.sum(values.reshape(-1, 8, DEPTH), axis=0)

    def total(values):
        return jnp.sum(values, keepdims=True)

    def spread_groups(turn, value):
        ysc[turn, group] = jnp.broadcast_to(value, (8, 128))
        for step in range(1, GROUPS):
            peer = lax.rem(group + step, GROUPS)
            pltpu.make_async_remote_copy(
                src_ref=ysc.at[turn, group], dst_ref=ysc.at[turn, group],
                send_sem=ys_send.at[turn], recv_sem=ys_recv.at[turn],
                device_id=(me, peer), device_id_type=MESH,
            ).start()

    def spread_slabs(turn, values):
        settle(ysc.at[turn, pl.ds(0, GROUPS - 1)], ys_recv.at[turn])
        sums = jnp.sum(ysc[turn], axis=0)
        lane = lax.broadcasted_iota(jnp.int32, (8, 128), 1)
        for index, value in enumerate(values):
            sums = jnp.where(lane == index + 1, jnp.broadcast_to(value, (8, 128)), sums)
        tile[turn] = sums
        zsc[turn, me] = sums

        def send(step, carry):
            peer = lax.rem(me + step, SLABS)
            pltpu.make_async_remote_copy(
                src_ref=tile.at[turn, pl.ds(0, 1)], dst_ref=zsc.at[turn, me, pl.ds(0, 1)],
                send_sem=zs_send.at[turn], recv_sem=zs_recv.at[turn],
                device_id=(peer, group), device_id_type=MESH,
            ).start()
            return carry

        lax.fori_loop(1, SLABS, send, 0)

    def collect(turn):
        settle(zsc.at[turn, pl.ds(0, SLABS - 1), pl.ds(0, 1)], zs_recv.at[turn])
        summed = jnp.sum(zsc[turn, :, 0:1, :], axis=0)
        return [summed[:, index:index + 1] for index in range(3)]

    def front(turn, chunk):
        receive_chunk(turn, chunk)
        pr, pi = image(0, chunk)
        if turn == 1:
            ar, ai = image(1, chunk)
            ar, ai = ar + RIDGE * pr, ai + RIDGE * pi
            pr, pi = pr - alpha * ar, pi - alpha * ai
            acc[turn, 1] += fold_rows(pr * ar + pi * ai)
        acc[turn, 0] += fold_rows(pr * pr + pi * pi)
        if turn == 1:
            send_rows(1, chunk)
        for coil in range(COILS):
            sr, si = maps_of(coil, chunk)
            rows = pl.ds(coil * CHUNK, CHUNK)
            lhs[rows, :DEPTH] = (sr * pr - si * pi).astype(BF16)
            lhs[rows, DEPTH:] = (sr * pi + si * pr).astype(BF16)
        out = dot(lhs[...], df[...])
        for coil in range(COILS):
            rows = slice(coil * CHUNK, (coil + 1) * CHUNK)
            zbuf[coil, pl.ds(chunk * CHUNK, CHUNK), :] = out[rows, :DEPTH].astype(BF16)
            zbuf[coil, pl.ds(ROWS + chunk * CHUNK, CHUNK), :] = out[rows, DEPTH:].astype(BF16)

    zero = jnp.zeros((8, DEPTH), F32)
    acc[...] = jnp.zeros_like(acc)

    def arrivals(step, carry):
        @pl.when(step == 0)
        def _():
            settle(sb.at[:, pl.ds(0, BLOCKS - 1)], sb_recv.at[my_chunk])

        @pl.when((step > 0) & (step < CHUNKS))
        def _():
            settle(sb.at[:, pl.ds(0, BLOCKS)], sb_recv.at[turn_order(step)])

        @pl.when(step < CHUNKS)
        def _():
            combine(0, turn_order(step))

        @pl.when((step >= 1) & (step < CHUNKS + 1))
        def _():
            second_step(0, turn_order(step - 1))

        @pl.when((step >= 2) & (step < CHUNKS + 2))
        def _():
            third_step(0, turn_order(step - 2))

        @pl.when(step >= 3)
        def _():
            front(0, turn_order(step - 3))

        return carry

    lax.fori_loop(0, CHUNKS + 3, arrivals, 0)

    alpha = None
    for turn in range(2):
        if turn == 1:
            over_chunks(front, 1)

        def rows_coil(coil, energy):
            if turn == 0:
                send_rows(0, turn_order(coil))
            for half in range(2):
                out = dot(rf[half * ROWS:(half + 1) * ROWS, :], zbuf[coil])
                weighted = out.astype(BF16) * mask[...]
                mbuf[coil, half * ROWS:(half + 1) * ROWS, :] = weighted
                wide = weighted.astype(F32)
                energy = energy + fold_rows(wide * wide)
            return energy

        energy = lax.fori_loop(0, COILS, rows_coil, zero)
        spread_groups(turn, total(energy))
        over_chunks(combine, turn + 1)
        spread_slabs(turn, (total(acc[turn, 0]), total(acc[turn, 1])))
        over_chunks(second_step, turn + 1)
        over_chunks(third_step, turn + 1)
        if turn == 0:
            spectral, norm0, _ = collect(0)
            energy0 = spectral + RIDGE * norm0
            alpha = norm0 / energy0

    for turn in range(2):
        rowbuf[turn, me] = cs[turn, my_place]
        settle(rowbuf.at[turn, pl.ds(0, SLABS - 1)], rb_recv.at[turn])
    first, second, half = route(my_chunk)
    rowbuf[2, me, :, columns(half)] = cs[2, my_place, :, columns(half)]
    settle(rowbuf.at[2, pl.ds(0, SLABS - 1), :, columns(half)], rb_recv.at[2])

    def swap(step, carry):
        some = pl.ds(step * 16, 16)
        pltpu.make_async_remote_copy(
            src_ref=rowbuf.at[2, some, :, columns(half)], dst_ref=rowbuf.at[2, some, :, columns(half)],
            send_sem=last_send, recv_sem=last_recv.at[step],
            device_id=(me, first), device_id_type=MESH,
        ).start()
        return carry

    lax.fori_loop(0, SLABS // 16, swap, 0)
    spectral, norm1, cross1 = collect(1)
    beta = norm1 / norm0
    energy1 = spectral + RIDGE * norm1 + 2.0 * beta * cross1 + beta * beta * energy0
    alpha1 = norm1 / energy1
    def finish(step, carry):
        some = pl.ds(step * 16, 16)
        settle(rowbuf.at[2, some, :, columns(1 - half)], last_recv.at[step])
        start = rowbuf[0, some].astype(F32)
        applied = rowbuf[1, some].astype(F32) + RIDGE * start
        residual = start - alpha * applied
        again = rowbuf[2, some].astype(F32) + RIDGE * residual
        direction = residual + beta * start
        answer = alpha * start + alpha1 * direction
        left = residual - alpha1 * (again + beta * applied)
        for index in range(2):
            sol_ref[index, some] = answer[:, index * 8:index * 8 + 8]
            res_ref[index, some] = left[:, index * 8:index * 8 + 8]
        return carry

    lax.fori_loop(0, SLABS // 16, finish, 0)

    settle(kd.at[:, :, pl.ds(0, CHUNK * 3), :], kd_send)
    for phase in range(2, CHUNKS):
        maps_left(phase)
    for turn in range(3):
        settle(got1.at[turn], p1_send.at[turn])
        settle(got1.at[turn], p2_send.at[turn])
    for turn in range(2):
        settle(got1.at[turn], p3_send.at[turn])
        settle(rowbuf.at[turn, pl.ds(0, SLABS - 1)], rb_send.at[turn])
    settle(rowbuf.at[2, pl.ds(0, SLABS - 1), :, columns(half)], rb_send.at[2])
    settle(rowbuf.at[2, :, :, columns(half)], last_send)
    for turn in range(2):
        settle(ysc.at[turn, pl.ds(0, GROUPS - 1)], ys_send.at[turn])
        settle(zsc.at[turn, pl.ds(0, SLABS - 1), pl.ds(0, 1)], zs_send.at[turn])


def shards(raw_data, gcc_matrix, sens_maps, line_mask):
    gcc = gcc_matrix.reshape(2, 16, 64)
    raw = raw_data.reshape(2 * 64, ROWS // GROUPS, DEPTH)
    maps = jnp.transpose(sens_maps, (1, 2, 0, 3, 4)).reshape(COILS, SLABS, 16, DEPTH)

    dma = pltpu.SemaphoreType.DMA
    out = jax.ShapeDtypeStruct((2, SLABS, 8, DEPTH), F32)
    return pl.pallas_call(
        kernel,
        out_shape=(out, out),
        in_specs=[pl.BlockSpec(memory_space=pltpu.VMEM)] + [pl.BlockSpec(memory_space=pl.ANY)] * 7,
        out_specs=(pl.BlockSpec(memory_space=pltpu.VMEM),) * 2,
        scratch_shapes=[
            pltpu.VMEM((SLICES, 2 * 64, SLICE, DEPTH), BF16),
            pltpu.VMEM((2 * 16 * SLICE, 2 * 64 * SLICE), BF16),
            pltpu.VMEM((2, 16, ROWS // GROUPS, DEPTH), BF16),
            pltpu.VMEM((ROWS, DEPTH), jnp.int32),
            pltpu.VMEM((2, 2, 8, DEPTH), F32),
            pltpu.VMEM((2, COILS, ROWS, DEPTH), BF16),
            pltpu.VMEM((COILS, SLABS, 16, DEPTH), BF16),
            pltpu.VMEM((ROWS, DEPTH), BF16),
            pltpu.VMEM((2 * ROWS, 2 * ROWS), BF16),
            pltpu.VMEM((2 * ROWS, 2 * ROWS), BF16),
            pltpu.VMEM((2 * DEPTH, 2 * DEPTH), BF16),
            pltpu.VMEM((2 * DEPTH, 2 * DEPTH), BF16),
            pltpu.VMEM((COILS, 2 * ROWS, DEPTH), BF16),
            pltpu.VMEM((COILS, 2 * ROWS, DEPTH), BF16),
            pltpu.VMEM((CHUNKS, COILS * CHUNK, 2 * DEPTH), F32),
            pltpu.VMEM((COILS * CHUNK, 2 * DEPTH), BF16),
            pltpu.VMEM((3, SLABS, 16, DEPTH), BF16),
            pltpu.VMEM((3, CHUNKS, BLOCKS, 16, 128), BF16),
            pltpu.VMEM((3, CHUNKS, BLOCKS, 16, 128), BF16),
            pltpu.VMEM((3, CHUNKS, BLOCKS, 16, 128), BF16),
            pltpu.VMEM((3, SLABS, 16, DEPTH), BF16),
            pltpu.VMEM((3, SLABS, 16, DEPTH), BF16),
            pltpu.VMEM((2, GROUPS, 8, 128), F32),
            pltpu.VMEM((2, SLABS, 8, 128), F32),
            pltpu.VMEM((2, 8, 128), F32),
            dma((SLICES,)), dma((6,)), dma, dma, dma((CHUNKS,)), dma((CHUNKS,)),
            dma((3,)), dma((3, CHUNKS)), dma((3,)), dma((3, CHUNKS)), dma((2,)), dma((2, CHUNKS)),
            dma((3,)), dma((3,)), dma, dma((SLABS // 16,)), dma((2,)), dma((2,)), dma((2,)), dma((2,)),
        ],
        compiler_params=pltpu.CompilerParams(
            collective_id=0, has_side_effects=True, vmem_limit_bytes=48 * 1024 * 1024
        ),
    )(gcc, raw, maps, line_mask, *tables())


def solution(mesh):
    placed = (
        P(None, None, "slab", "coil", None),
        P(None, "slab", None, None),
        P(None, "coil", None, "slab", None),
        P(),
    )
    return jax.shard_map(
        shards,
        mesh=mesh,
        in_specs=placed,
        out_specs=(P(None, None, "slab", None), P(None, None, "slab", None)),
        check_vma=False,
    )
```

```python
import math

import jax
import jax.numpy as jnp
import ml_dtypes
import numpy as np
from jax import lax
from jax.experimental import pallas as pl
from jax.experimental.pallas import tpu as pltpu
from jax.sharding import PartitionSpec as P

MESH = pl.DeviceIdType.MESH
BF16 = jnp.bfloat16
F32 = jnp.float32

RIDGE = 0.5
SLABS = 64
GROUPS = 4
COILS = 4
ROWS = 512
DEPTH = 256
CHUNKS = 4
CHUNK = ROWS // CHUNKS
SLICE = 16
SLICES = ROWS // GROUPS // SLICE
BLOCKS = SLABS // CHUNKS


def place(slab):
    z, x, core = lax.div(slab, 8), lax.rem(lax.div(slab, 2), 4), lax.rem(slab, 2)
    return lax.rem(z + x, 2) * 2 + core, z * 2 + lax.div(x, 2)


def member(chunk, index):
    z = lax.div(index, 2)
    x = 2 * lax.rem(index, 2) + lax.rem(z + lax.div(chunk, 2), 2)
    return z * 8 + x * 2 + lax.rem(chunk, 2)


def tables():
    def cos_sin(length):
        index = np.arange(length, dtype=np.int64)
        angle = (index[:, None] * index[None, :] % length) * (2.0 * math.pi / length)
        return np.cos(angle) / math.sqrt(length), np.sin(angle) / math.sqrt(length)

    slab = np.arange(SLABS)
    z, x, core = slab // 8, slab // 2 % 4, slab % 2
    position = ((z + x) % 2 * 2 + core) * BLOCKS + z * 2 + x // 2
    order = np.zeros(SLABS, np.int64)
    order[position] = slab
    rows = (order[:, None] * 8 + np.arange(8)[None, :]).reshape(-1)
    cosine, sine = cos_sin(ROWS)
    cosine, sine = cosine[:, rows], sine[:, rows]
    rows_forward = np.block([[cosine, sine], [-sine, cosine]])
    rows_inverse = np.block([[cosine.T, -sine.T], [sine.T, cosine.T]])
    rows_inverse = rows_inverse.reshape(2, CHUNKS, CHUNK, 2 * ROWS).swapaxes(0, 1).reshape(2 * ROWS, 2 * ROWS)
    cosine, sine = cos_sin(DEPTH)
    depth_forward = np.block([[cosine, -sine], [sine, cosine]])
    depth_inverse = np.block([[cosine, sine], [-sine, cosine]])
    return [
        jnp.asarray(table.astype(ml_dtypes.bfloat16))
        for table in (rows_forward, rows_inverse, depth_forward, depth_inverse)
    ]


def dot(left, right):
    return jnp.dot(left, right, preferred_element_type=F32)


def kernel(
    gcc, raw_hbm, sens_hbm, mask_hbm, rf_hbm, ri_hbm, df_hbm, di_hbm,
    sol_ref, res_ref,
    raw, mix, comp, whole_mask, acc,
    kd, sb, mask, rf, ri, df, di,
    zbuf, mbuf, early, lhs,
    part, got1, sum1, got2, cs, rowbuf,
    ysc, zsc, tile,
    raw_sem, load_sem, kd_send, kd_recv, sb_send, sb_recv,
    p1_send, p1_recv, p2_send, p2_recv, p3_send, p3_recv,
    rb_send, rb_recv, last_send, last_recv, ys_send, ys_recv, zs_send, zs_recv,
):
    me = lax.axis_index("slab")
    group = lax.axis_index("coil")
    my_chunk, my_index = place(me)
    my_place = my_chunk * BLOCKS + my_index
    side_a = group + 1 - 2 * lax.rem(group, 2)
    side_b = 3 - group
    half_a = lax.rem(lax.div(group + 1, 2), 2)
    half_b = lax.div(group, 2)

    barrier = pltpu.get_barrier_semaphore()

    def greet(step, carry):
        peer = lax.rem(me + step, SLABS)
        pl.semaphore_signal(barrier, inc=1, device_id=(peer, group), device_id_type=MESH)
        return carry

    lax.fori_loop(1, SLABS, greet, 0)
    for step in range(1, GROUPS):
        pl.semaphore_signal(
            barrier, inc=1, device_id=(me, lax.rem(group + step, GROUPS)), device_id_type=MESH
        )

    maps_load = pltpu.make_async_copy(sens_hbm.at[:, me], sb.at[:, my_place], load_sem.at[0])
    mask_load = pltpu.make_async_copy(mask_hbm, whole_mask, load_sem.at[1])
    rows_load = pltpu.make_async_copy(ri_hbm, ri, load_sem.at[2])
    late_loads = [
        maps_load,
        pltpu.make_async_copy(di_hbm, di, load_sem.at[3]),
        pltpu.make_async_copy(df_hbm, df, load_sem.at[4]),
        pltpu.make_async_copy(rf_hbm, rf, load_sem.at[5]),
    ]

    def raw_load(step):
        return pltpu.make_async_copy(
            raw_hbm.at[:, pl.ds(step * SLICE, SLICE), :], raw.at[step], raw_sem.at[step]
        )

    def start_raw(step, carry):
        raw_load(step).start()
        return carry

    lax.fori_loop(0, SLICES, start_raw, 0)
    for load in [mask_load, rows_load] + late_loads:
        load.start()

    pl.semaphore_wait(barrier, SLABS - 1 + GROUPS - 1)

    def settle(ref, sem):
        pltpu.make_async_copy(ref, ref, sem).wait()

    def send_maps(phase):
        chunk = lax.rem(my_chunk + phase, CHUNKS)

        def send(step, carry):
            peer = member(chunk, lax.rem(my_index + 5 * step, BLOCKS))
            pltpu.make_async_remote_copy(
                src_ref=sens_hbm.at[:, peer], dst_ref=sb.at[:, my_place],
                send_sem=sb_send.at[phase], recv_sem=sb_recv.at[my_chunk],
                device_id=(peer, group), device_id_type=MESH,
            ).start()
            return carry

        lax.fori_loop(0 if phase else 1, BLOCKS, send, 0)

    def maps_left(phase):
        settle(sb.at[:, pl.ds(0, BLOCKS if phase else BLOCKS - 1)], sb_send.at[phase])

    send_maps(0)
    send_maps(1)

    def turn_order(step):
        return lax.rem(my_chunk + CHUNKS - step, CHUNKS)

    def same(shape, left, right):
        one = lax.broadcasted_iota(jnp.int32, shape, 0)
        two = lax.broadcasted_iota(jnp.int32, shape, 1)
        return left(one) == right(two)

    up = same((16 * SLICE, 16), lambda a: a // SLICE, lambda b: b).astype(F32).astype(BF16)
    across = same((64, 64 * SLICE), lambda a: a, lambda b: b // SLICE).astype(F32).astype(BF16)
    diagonal = same((16 * SLICE, 64 * SLICE), lambda a: a % SLICE, lambda b: b % SLICE)
    real, imag = [
        jnp.where(diagonal, dot(dot(up, gcc[index]).astype(BF16), across), 0.0) for index in range(2)
    ]
    tall, wide = 16 * SLICE, 64 * SLICE
    mix[:tall, :wide] = real.astype(BF16)
    mix[:tall, wide:] = (-imag).astype(BF16)
    mix[tall:, :wide] = imag.astype(BF16)
    mix[tall:, wide:] = real.astype(BF16)

    def compress(step, carry):
        raw_load(step).wait()
        out = dot(mix[...], raw[step].reshape(2 * wide, DEPTH))
        here = pl.ds(step * SLICE, SLICE)
        there = pl.ds(CHUNK * group + step * SLICE, SLICE)
        comp[:, :, here, :] = out.astype(BF16).reshape(2, 16, SLICE, DEPTH)
        kd[:, :, there, :] = comp[:, pl.ds(COILS * group, COILS), here, :]
        for shift in range(1, GROUPS):
            peer = lax.rem(group + shift, GROUPS)
            pltpu.make_async_remote_copy(
                src_ref=comp.at[:, pl.ds(COILS * peer, COILS), here, :],
                dst_ref=kd.at[:, :, there, :],
                send_sem=kd_send, recv_sem=kd_recv,
                device_id=(me, peer), device_id_type=MESH,
            ).start()
        return carry

    lax.fori_loop(0, SLICES, compress, 0)
    for phase in range(2):
        maps_left(phase)
        send_maps(phase + 2)
    mask_load.wait()
    mask[...] = whole_mask[...].astype(F32).astype(BF16)
    rows_load.wait()
    settle(kd.at[:, :, pl.ds(0, CHUNK * 3), :], kd_recv)

    def inverse(chunk):
        def coil_rows(coil, carry):
            out = dot(ri[pl.ds(chunk * 2 * CHUNK, 2 * CHUNK), :], mbuf[coil]).astype(BF16)
            rows = pl.ds(pl.multiple_of(coil * CHUNK, CHUNK), CHUNK)
            lhs[rows, :DEPTH] = out[:CHUNK]
            lhs[rows, DEPTH:] = out[CHUNK:]
            return carry

        lax.fori_loop(0, COILS, coil_rows, 0, unroll=True)
        return dot(lhs[...], di[...])

    for load in late_loads:
        load.wait()

    def data_coil(coil, carry):
        for half in range(2):
            mbuf[coil, half * ROWS:(half + 1) * ROWS, :] = kd[half, coil] * mask[...]
        return carry

    lax.fori_loop(0, COILS, data_coil, 0)

    def data_chunk(chunk, carry):
        early[chunk] = inverse(chunk)
        return carry

    lax.fori_loop(0, CHUNKS, data_chunk, 0)

    def maps_of(coil, chunk):
        both = sb[coil, pl.ds(chunk * BLOCKS, BLOCKS)].astype(F32)
        return both[:, :8].reshape(CHUNK, DEPTH), both[:, 8:].reshape(CHUNK, DEPTH)

    def route(chunk):
        odd = lax.rem(chunk, 2)
        first = side_a + odd * (side_b - side_a)
        second = side_b + odd * (side_a - side_b)
        return first, second, half_a + odd * (half_b - half_a)

    def columns(half):
        return pl.ds(pl.multiple_of(half * 128, 128), 128)

    def blocks(chunk):
        return pl.ds(chunk * BLOCKS, BLOCKS)

    def combine(turn, chunk):
        out = early[chunk] if turn == 0 else inverse(chunk)
        real = imag = None
        for coil in range(COILS):
            a = out[coil * CHUNK:(coil + 1) * CHUNK, :DEPTH]
            b = out[coil * CHUNK:(coil + 1) * CHUNK, DEPTH:]
            sr, si = maps_of(coil, chunk)
            re, im = sr * a + si * b, sr * b - si * a
            real = re if real is None else real + re
            imag = im if imag is None else imag + im
        packed = jnp.concatenate(
            [real.reshape(BLOCKS, 8, DEPTH), imag.reshape(BLOCKS, 8, DEPTH)], axis=1
        )
        part[turn, blocks(chunk)] = packed.astype(BF16)
        first, second, half = route(chunk)
        pltpu.make_async_remote_copy(
            src_ref=part.at[turn, blocks(chunk), :, columns(1 - half)],
            dst_ref=got1.at[turn, chunk],
            send_sem=p1_send.at[turn], recv_sem=p1_recv.at[turn, chunk],
            device_id=(me, first), device_id_type=MESH,
        ).start()

    def second_step(turn, chunk):
        first, second, half = route(chunk)
        settle(got1.at[turn, chunk], p1_recv.at[turn, chunk])
        mine = part[turn, blocks(chunk), :, columns(half)].astype(F32)
        sum1[turn, chunk] = (mine + got1[turn, chunk].astype(F32)).astype(BF16)
        pltpu.make_async_remote_copy(
            src_ref=sum1.at[turn, chunk], dst_ref=got2.at[turn, chunk],
            send_sem=p2_send.at[turn], recv_sem=p2_recv.at[turn, chunk],
            device_id=(me, second), device_id_type=MESH,
        ).start()

    def third_step(turn, chunk):
        first, second, half = route(chunk)
        settle(got2.at[turn, chunk], p2_recv.at[turn, chunk])
        whole = sum1[turn, chunk].astype(F32) + got2[turn, chunk].astype(F32)
        cs[turn, blocks(chunk), :, columns(half)] = whole.astype(BF16)
        if turn == 2:
            send_rows(turn, chunk, columns(half))
            return
        pltpu.make_async_remote_copy(
            src_ref=cs.at[turn, blocks(chunk), :, columns(half)],
            dst_ref=cs.at[turn, blocks(chunk), :, columns(half)],
            send_sem=p3_send.at[turn], recv_sem=p3_recv.at[turn, chunk],
            device_id=(me, first), device_id_type=MESH,
        ).start()

    def over_chunks(work, turn):
        def step(index, carry):
            work(turn, turn_order(index))
            return carry

        lax.fori_loop(0, CHUNKS, step, 0)

    def receive_chunk(turn, chunk):
        first, second, half = route(chunk)
        settle(cs.at[turn, blocks(chunk), :, columns(1 - half)], p3_recv.at[turn, chunk])

    def send_rows(turn, chunk, lanes=slice(None)):
        def send(step, carry):
            to = lax.rem(my_index + step, BLOCKS)
            peer = member(chunk, to)

            @pl.when(peer != me)
            def _():
                pltpu.make_async_remote_copy(
                    src_ref=cs.at[turn, chunk * BLOCKS + to, :, lanes],
                    dst_ref=rowbuf.at[turn, me, :, lanes],
                    send_sem=rb_send.at[turn], recv_sem=rb_recv.at[turn],
                    device_id=(peer, group), device_id_type=MESH,
                ).start()

            return carry

        lax.fori_loop(0, BLOCKS, send, 0)

    def image(turn, chunk):
        both = cs[turn, pl.ds(chunk * BLOCKS, BLOCKS)].astype(F32)
        return both[:, :8].reshape(CHUNK, DEPTH), both[:, 8:].reshape(CHUNK, DEPTH)

    def fold_rows(values):
        return jnp.sum(values.reshape(-1, 8, DEPTH), axis=0)

    def total(values):
        return jnp.sum(values, keepdims=True)

    def spread_groups(turn, value):
        ysc[turn, group] = jnp.broadcast_to(value, (8, 128))
        for step in range(1, GROUPS):
            peer = lax.rem(group + step, GROUPS)
            pltpu.make_async_remote_copy(
                src_ref=ysc.at[turn, group], dst_ref=ysc.at[turn, group],
                send_sem=ys_send.at[turn], recv_sem=ys_recv.at[turn],
                device_id=(me, peer), device_id_type=MESH,
            ).start()

    def spread_slabs(turn, values):
        settle(ysc.at[turn, pl.ds(0, GROUPS - 1)], ys_recv.at[turn])
        sums = jnp.sum(ysc[turn], axis=0)
        lane = lax.broadcasted_iota(jnp.int32, (8, 128), 1)
        for index, value in enumerate(values):
            sums = jnp.where(lane == index + 1, jnp.broadcast_to(value, (8, 128)), sums)
        tile[turn] = sums
        zsc[turn, me] = sums

        def send(step, carry):
            peer = lax.rem(me + step, SLABS)
            pltpu.make_async_remote_copy(
                src_ref=tile.at[turn, pl.ds(0, 1)], dst_ref=zsc.at[turn, me, pl.ds(0, 1)],
                send_sem=zs_send.at[turn], recv_sem=zs_recv.at[turn],
                device_id=(peer, group), device_id_type=MESH,
            ).start()
            return carry

        lax.fori_loop(1, SLABS, send, 0)

    def collect(turn):
        settle(zsc.at[turn, pl.ds(0, SLABS - 1), pl.ds(0, 1)], zs_recv.at[turn])
        summed = jnp.sum(zsc[turn, :, 0:1, :], axis=0)
        return [summed[:, index:index + 1] for index in range(3)]

    def front(turn, chunk):
        receive_chunk(turn, chunk)
        pr, pi = image(0, chunk)
        if turn == 1:
            ar, ai = image(1, chunk)
            ar, ai = ar + RIDGE * pr, ai + RIDGE * pi
            pr, pi = pr - alpha * ar, pi - alpha * ai
            acc[turn, 1] += fold_rows(pr * ar + pi * ai)
        acc[turn, 0] += fold_rows(pr * pr + pi * pi)
        send_rows(turn, chunk)
        for coil in range(COILS):
            sr, si = maps_of(coil, chunk)
            rows = pl.ds(coil * CHUNK, CHUNK)
            lhs[rows, :DEPTH] = (sr * pr - si * pi).astype(BF16)
            lhs[rows, DEPTH:] = (sr * pi + si * pr).astype(BF16)
        out = dot(lhs[...], df[...])
        for coil in range(COILS):
            rows = slice(coil * CHUNK, (coil + 1) * CHUNK)
            zbuf[coil, pl.ds(chunk * CHUNK, CHUNK), :] = out[rows, :DEPTH].astype(BF16)
            zbuf[coil, pl.ds(ROWS + chunk * CHUNK, CHUNK), :] = out[rows, DEPTH:].astype(BF16)

    zero = jnp.zeros((8, DEPTH), F32)
    acc[...] = jnp.zeros_like(acc)

    def arrivals(step, carry):
        @pl.when(step == 0)
        def _():
            settle(sb.at[:, pl.ds(0, BLOCKS - 1)], sb_recv.at[my_chunk])

        @pl.when((step > 0) & (step < CHUNKS))
        def _():
            settle(sb.at[:, pl.ds(0, BLOCKS)], sb_recv.at[turn_order(step)])

        @pl.when(step < CHUNKS)
        def _():
            combine(0, turn_order(step))

        @pl.when((step >= 1) & (step < CHUNKS + 1))
        def _():
            second_step(0, turn_order(step - 1))

        @pl.when((step >= 2) & (step < CHUNKS + 2))
        def _():
            third_step(0, turn_order(step - 2))

        @pl.when(step >= 3)
        def _():
            front(0, turn_order(step - 3))

        return carry

    lax.fori_loop(0, CHUNKS + 3, arrivals, 0)

    alpha = None
    for turn in range(2):
        if turn == 1:
            over_chunks(front, 1)

        def rows_coil(coil, energy):
            for half in range(2):
                out = dot(rf[half * ROWS:(half + 1) * ROWS, :], zbuf[coil])
                weighted = out.astype(BF16) * mask[...]
                mbuf[coil, half * ROWS:(half + 1) * ROWS, :] = weighted
                wide = weighted.astype(F32)
                energy = energy + fold_rows(wide * wide)
            return energy

        energy = lax.fori_loop(0, COILS, rows_coil, zero)
        spread_groups(turn, total(energy))
        over_chunks(combine, turn + 1)
        spread_slabs(turn, (total(acc[turn, 0]), total(acc[turn, 1])))
        over_chunks(second_step, turn + 1)
        over_chunks(third_step, turn + 1)
        if turn == 0:
            spectral, norm0, _ = collect(0)
            energy0 = spectral + RIDGE * norm0
            alpha = norm0 / energy0

    for turn in range(2):
        rowbuf[turn, me] = cs[turn, my_place]
        settle(rowbuf.at[turn, pl.ds(0, SLABS - 1)], rb_recv.at[turn])
    first, second, half = route(my_chunk)
    rowbuf[2, me, :, columns(half)] = cs[2, my_place, :, columns(half)]
    settle(rowbuf.at[2, pl.ds(0, SLABS - 1), :, columns(half)], rb_recv.at[2])

    def swap(step, carry):
        some = pl.ds(step * 16, 16)
        pltpu.make_async_remote_copy(
            src_ref=rowbuf.at[2, some, :, columns(half)], dst_ref=rowbuf.at[2, some, :, columns(half)],
            send_sem=last_send, recv_sem=last_recv.at[step],
            device_id=(me, first), device_id_type=MESH,
        ).start()
        return carry

    lax.fori_loop(0, SLABS // 16, swap, 0)
    spectral, norm1, cross1 = collect(1)
    beta = norm1 / norm0
    energy1 = spectral + RIDGE * norm1 + 2.0 * beta * cross1 + beta * beta * energy0
    alpha1 = norm1 / energy1
    def finish(step, carry):
        some = pl.ds(step * 16, 16)
        settle(rowbuf.at[2, some, :, columns(1 - half)], last_recv.at[step])
        start = rowbuf[0, some].astype(F32)
        applied = rowbuf[1, some].astype(F32) + RIDGE * start
        residual = start - alpha * applied
        again = rowbuf[2, some].astype(F32) + RIDGE * residual
        direction = residual + beta * start
        answer = alpha * start + alpha1 * direction
        left = residual - alpha1 * (again + beta * applied)
        for index in range(2):
            sol_ref[index, some] = answer[:, index * 8:index * 8 + 8]
            res_ref[index, some] = left[:, index * 8:index * 8 + 8]
        return carry

    lax.fori_loop(0, SLABS // 16, finish, 0)

    settle(kd.at[:, :, pl.ds(0, CHUNK * 3), :], kd_send)
    for phase in range(2, CHUNKS):
        maps_left(phase)
    for turn in range(3):
        settle(got1.at[turn], p1_send.at[turn])
        settle(got1.at[turn], p2_send.at[turn])
    for turn in range(2):
        settle(got1.at[turn], p3_send.at[turn])
        settle(rowbuf.at[turn, pl.ds(0, SLABS - 1)], rb_send.at[turn])
    settle(rowbuf.at[2, pl.ds(0, SLABS - 1), :, columns(half)], rb_send.at[2])
    settle(rowbuf.at[2, :, :, columns(half)], last_send)
    for turn in range(2):
        settle(ysc.at[turn, pl.ds(0, GROUPS - 1)], ys_send.at[turn])
        settle(zsc.at[turn, pl.ds(0, SLABS - 1), pl.ds(0, 1)], zs_send.at[turn])


def shards(raw_data, gcc_matrix, sens_maps, line_mask):
    gcc = gcc_matrix.reshape(2, 16, 64)
    raw = raw_data.reshape(2 * 64, ROWS // GROUPS, DEPTH)
    maps = jnp.transpose(sens_maps, (1, 2, 0, 3, 4)).reshape(COILS, SLABS, 16, DEPTH)

    dma = pltpu.SemaphoreType.DMA
    out = jax.ShapeDtypeStruct((2, SLABS, 8, DEPTH), F32)
    return pl.pallas_call(
        kernel,
        out_shape=(out, out),
        in_specs=[pl.BlockSpec(memory_space=pltpu.VMEM)] + [pl.BlockSpec(memory_space=pl.ANY)] * 7,
        out_specs=(pl.BlockSpec(memory_space=pltpu.VMEM),) * 2,
        scratch_shapes=[
            pltpu.VMEM((SLICES, 2 * 64, SLICE, DEPTH), BF16),
            pltpu.VMEM((2 * 16 * SLICE, 2 * 64 * SLICE), BF16),
            pltpu.VMEM((2, 16, ROWS // GROUPS, DEPTH), BF16),
            pltpu.VMEM((ROWS, DEPTH), jnp.int32),
            pltpu.VMEM((2, 2, 8, DEPTH), F32),
            pltpu.VMEM((2, COILS, ROWS, DEPTH), BF16),
            pltpu.VMEM((COILS, SLABS, 16, DEPTH), BF16),
            pltpu.VMEM((ROWS, DEPTH), BF16),
            pltpu.VMEM((2 * ROWS, 2 * ROWS), BF16),
            pltpu.VMEM((2 * ROWS, 2 * ROWS), BF16),
            pltpu.VMEM((2 * DEPTH, 2 * DEPTH), BF16),
            pltpu.VMEM((2 * DEPTH, 2 * DEPTH), BF16),
            pltpu.VMEM((COILS, 2 * ROWS, DEPTH), BF16),
            pltpu.VMEM((COILS, 2 * ROWS, DEPTH), BF16),
            pltpu.VMEM((CHUNKS, COILS * CHUNK, 2 * DEPTH), F32),
            pltpu.VMEM((COILS * CHUNK, 2 * DEPTH), BF16),
            pltpu.VMEM((3, SLABS, 16, DEPTH), BF16),
            pltpu.VMEM((3, CHUNKS, BLOCKS, 16, 128), BF16),
            pltpu.VMEM((3, CHUNKS, BLOCKS, 16, 128), BF16),
            pltpu.VMEM((3, CHUNKS, BLOCKS, 16, 128), BF16),
            pltpu.VMEM((3, SLABS, 16, DEPTH), BF16),
            pltpu.VMEM((3, SLABS, 16, DEPTH), BF16),
            pltpu.VMEM((2, GROUPS, 8, 128), F32),
            pltpu.VMEM((2, SLABS, 8, 128), F32),
            pltpu.VMEM((2, 8, 128), F32),
            dma((SLICES,)), dma((6,)), dma, dma, dma((CHUNKS,)), dma((CHUNKS,)),
            dma((3,)), dma((3, CHUNKS)), dma((3,)), dma((3, CHUNKS)), dma((2,)), dma((2, CHUNKS)),
            dma((3,)), dma((3,)), dma, dma((SLABS // 16,)), dma((2,)), dma((2,)), dma((2,)), dma((2,)),
        ],
        compiler_params=pltpu.CompilerParams(
            collective_id=0, has_side_effects=True, vmem_limit_bytes=48 * 1024 * 1024
        ),
    )(gcc, raw, maps, line_mask, *tables())


def solution(mesh):
    placed = (
        P(None, None, "slab", "coil", None),
        P(None, "slab", None, None),
        P(None, "coil", None, "slab", None),
        P(),
    )
    return jax.shard_map(
        shards,
        mesh=mesh,
        in_specs=placed,
        out_specs=(P(None, None, "slab", None), P(None, None, "slab", None)),
        check_vma=False,
    )
```
